32 devices in a mesh: body: 8 (over y, x, core), surf: 4 (over z).
Axes of the slice: x: 2, y: 2, z: 4, core: 2. Of those that a mesh axis runs over, the one named last changes fastest.
Arguments:
- body_panels: float32 [12, 24, 2048], P(None, 'body', 'surf'), may hold values from -6 to 48, as said below
- body_normals: float32 [3, 24, 2048], P(None, 'body', 'surf'), may hold values from -3 to 3
- fs_panels: float32 [4, 16384], P(None, ('body', 'surf')), may hold values from -6 to 48, as said below
- fs_state: float32 [2, 16384], P(None, ('body', 'surf')), may hold values from -6 to 6
- pairs: int32 [18, 2], replicated, may hold values from 0 to 23, as said below
Outputs:
- body_potential: float32 [24, 8, 2048], P('body', None, 'surf')
- body_force: float32 [24, 8, 3], P('body')
- fs_next: float32 [2, 16384], P(None, ('body', 'surf'))
The draws below stay inside these ranges and needn't reach their ends.
Inputs may be any that keep to these rules, and one draw needn't show every extreme that they name: Rows are distinct pairs (i, j) with i < j <= i + 3, ordered by i and then by j. `body_panels`: body b's centroids lie within x in 2 b - 1 to 2 b + 1, y in -1 to 1, z in -2 to -1; areas are positive; source strengths are within -6 to 6. `fs_panels`: Free-surface panels of group g have x in 2 * 3 g - 1 to 2 * 3 (g + 1) - 1, y in -3 to 3, positive areas, source strengths within -6 to 6.
All inputs are finite; a program needn't handle non-finite values.
Results may differ from the reference program's by a relative error of at most 0.0003.
Values sent between devices are 32-bit elements; how exact they have to be, the bound alone decides.
No kernel may reach another device: no remote copies, remote signals or barrier semaphores. Data moves between devices by JAX's collectives and lax.ppermute only.
A program may use at most 64 MiB of HBM per device.

```python
import math
import jax
import jax.numpy as jnp
from jax import lax

P_SIZE = 2048
SETS = 8
BODY_DEV = 3
FS = 2048
BODIES = 24
FS_ALL = 16384
NPAIRS = 18


def draw_body_panels(key, part):
    key_place, key_area, key_source = jax.random.split(key, 3)
    spread = jax.random.uniform(key_place, (3, BODIES, P_SIZE), jnp.float32, -1.0, 1.0)
    centre = 2.0 * jnp.arange(BODIES, dtype=jnp.float32)[:, None]
    coord_x = centre + spread[0]
    coord_y = spread[1]
    coord_z = -1.5 + 0.5 * spread[2]
    area = jax.random.uniform(key_area, (1, BODIES, P_SIZE), jnp.float32, 0.5, 1.5) * (4.0 / math.sqrt(P_SIZE))
    source = jnp.clip(jax.random.normal(key_source, (SETS, BODIES, P_SIZE), jnp.float32), -6.0, 6.0)
    return jnp.concatenate([coord_x[None], coord_y[None], coord_z[None], area, source], axis=0)


def draw_fs_panels(key, part):
    key_x, key_y, key_source, key_area = jax.random.split(key, 4)
    group = (jnp.arange(FS_ALL, dtype=jnp.int32) // FS).astype(jnp.float32)
    span = 2.0 * BODY_DEV
    coord_x = span * group + span * jax.random.uniform(key_x, (FS_ALL,), jnp.float32, 0.0, 1.0) - 1.0
    coord_y = jax.random.uniform(key_y, (FS_ALL,), jnp.float32, -3.0, 3.0)
    source = jnp.clip(jax.random.normal(key_source, (FS_ALL,), jnp.float32), -6.0, 6.0)
    area = jax.random.uniform(key_area, (FS_ALL,), jnp.float32, 0.5, 1.5) * (4.0 / math.sqrt(FS))
    return jnp.stack([coord_x, coord_y, source, area])


def draw_pairs(key, part):
    candidate_count = BODIES * BODY_DEV
    candidate = jnp.arange(candidate_count, dtype=jnp.int32)
    first_body = candidate // BODY_DEV
    reach_step = candidate % BODY_DEV + 1
    valid = first_body + reach_step < BODIES
    scores = jax.random.randint(key, (candidate_count,), 0, 1024, dtype=jnp.int32) * candidate_count + candidate + 2
    forced = (candidate == 0) | (candidate == (BODIES - 2) * BODY_DEV)
    scores = jnp.where(forced, candidate - candidate_count, scores)
    scores = jnp.where(valid, scores, 1025 * candidate_count + candidate + 2)
    chosen = jnp.sort(jnp.argsort(scores)[:NPAIRS])
    return jnp.stack([first_body[chosen], first_body[chosen] + reach_step[chosen]], axis=1).astype(jnp.int32)


def steps_of(own_key, extent, cuts, least, top_value):
    level, own = 1.0, jax.random.fold_in(own_key, 6)
    for position, blocks in cuts:
        heights = jnp.exp(jax.random.uniform(jax.random.fold_in(own, position), (blocks,), jnp.float32, least / len(cuts), top_value / len(cuts)))
        level = level * jnp.repeat(heights, extent[position] // blocks).reshape([-1 if axis == position else 1 for axis in range(len(extent))])
    return level


def noise(stream_key, shape, deviation, most, cuts=(), held_as=jnp.bfloat16):
    values = deviation * jax.random.normal(stream_key, shape, jnp.float32)
    if cuts:
        values = values * steps_of(stream_key, shape, cuts, -0.22, 0.18)
    return jnp.clip(values, -most, most).astype(held_as)


def setup_inputs(seed: int = 0) -> dict:
    arg_keys = jax.random.split(jax.random.key(seed), 6)
    return {
        "body_panels": draw_body_panels(jax.random.fold_in(arg_keys[5], 71), 0),
        "body_normals": noise(arg_keys[1], (3, BODIES, P_SIZE), 0.6, 3.0, ((1, 8), (2, 4)), jnp.float32),
        "fs_panels": draw_fs_panels(jax.random.fold_in(arg_keys[5], 71), 0),
        "fs_state": noise(arg_keys[3], (2, FS_ALL), 1.0, 6.0, ((1, 32),), jnp.float32),
        "pairs": draw_pairs(jax.random.fold_in(arg_keys[5], 71), 0),
    }


soften = 0.01
gravity = 9.81
time_step = 0.2
highest = lax.Precision.HIGHEST

def kernel_block(targets, sources):
    delta_x = targets[0][:, None] - sources[0][None, :]
    delta_y = targets[1][:, None] - sources[1][None, :]
    delta_z = targets[2][:, None] - sources[2][None, :]
    return lax.rsqrt(delta_x * delta_x + delta_y * delta_y + delta_z * delta_z + soften)

def reference(body_panels, body_normals, fs_panels, fs_state, pairs):
    points = body_panels[:3]
    weights = body_panels[4:] * body_panels[3][None]

    def self_term(body_id):
        body_points = lax.dynamic_index_in_dim(points, body_id, 1, keepdims=False)
        body_weights = lax.dynamic_index_in_dim(weights, body_id, 1, keepdims=False)
        influence = kernel_block(body_points, body_points)
        return lax.dot_general(body_weights, influence, (((1,), (1,)), ((), ())), precision=highest)
    potential = lax.map(self_term, jnp.arange(BODIES, dtype=jnp.int32))

    def pair_step(acc_potential, pair_row):
        first_body = pair_row[0]
        second_body = pair_row[1]
        first_points = lax.dynamic_index_in_dim(points, first_body, 1, keepdims=False)
        second_points = lax.dynamic_index_in_dim(points, second_body, 1, keepdims=False)
        first_weights = lax.dynamic_index_in_dim(weights, first_body, 1, keepdims=False)
        second_weights = lax.dynamic_index_in_dim(weights, second_body, 1, keepdims=False)
        influence = kernel_block(first_points, second_points)
        to_first = lax.dot_general(second_weights, influence, (((1,), (1,)), ((), ())), precision=highest)
        to_second = jnp.dot(first_weights, influence, precision=highest)
        acc_potential = acc_potential.at[first_body].add(to_first)
        acc_potential = acc_potential.at[second_body].add(to_second)
        return (acc_potential, None)
    potential, unused = lax.scan(pair_step, potential, pairs)
    groups = BODIES // BODY_DEV
    fs_points = jnp.stack([fs_panels[0], fs_panels[1], jnp.zeros_like(fs_panels[0])])
    fs_weights = fs_panels[2] * fs_panels[3]

    def group_term(group_id):
        group_points = lax.dynamic_slice_in_dim(points, group_id * BODY_DEV, BODY_DEV, 1).reshape(3, BODY_DEV * P_SIZE)
        group_weights = lax.dynamic_slice_in_dim(weights[0], group_id * BODY_DEV, BODY_DEV, 0).reshape(BODY_DEV * P_SIZE)
        surface_points = lax.dynamic_slice_in_dim(fs_points, group_id * FS, FS, 1)
        surface_weights = lax.dynamic_slice_in_dim(fs_weights, group_id * FS, FS, 0)
        delta_x = surface_points[0][None, :] - group_points[0][:, None]
        delta_y = surface_points[1][None, :] - group_points[1][:, None]
        delta_z = surface_points[2][None, :] - group_points[2][:, None]
        inverse = lax.rsqrt(delta_x * delta_x + delta_y * delta_y + delta_z * delta_z + soften)
        from_surface = jnp.dot(inverse, surface_weights, precision=highest).reshape(BODY_DEV, P_SIZE)
        cubed = inverse * inverse * inverse
        velocity = -jnp.stack([jnp.dot(group_weights, delta_x * cubed, precision=highest), jnp.dot(group_weights, delta_y * cubed, precision=highest), jnp.dot(group_weights, delta_z * cubed, precision=highest)])
        return (from_surface, velocity)
    from_surface, velocity = lax.map(group_term, jnp.arange(groups, dtype=jnp.int32))
    potential = potential.at[:, 0].add(from_surface.reshape(BODIES, P_SIZE))
    area_normals = body_normals * body_panels[3][None]
    force = jnp.einsum('cbp,bsp->bsc', area_normals, potential, precision=highest)
    velocity = velocity.transpose(1, 0, 2).reshape(3, FS_ALL)
    speed_sq = velocity[0] * velocity[0] + velocity[1] * velocity[1] + velocity[2] * velocity[2]
    next_potential = fs_state[0] + time_step * (-gravity * fs_state[1] - 0.5 * speed_sq)
    next_elevation = fs_state[1] + time_step * velocity[2]
    return (potential, force, jnp.stack([next_potential, next_elevation]))
```

```python
import functools

import jax
import jax.numpy as jnp
from jax import lax
from jax.experimental import pallas as pl
from jax.experimental.pallas import tpu as pltpu
from jax.sharding import PartitionSpec as P

soften = 0.01
gravity = 9.81
time_step = 0.2
mid_depth = -1.5
half = jnp.bfloat16
full = jnp.float32
DEPTH = 48


def rows_of(block_shape, rows):
    index = lax.broadcasted_iota(jnp.int32, block_shape, 0)
    block = jnp.zeros(block_shape, full)
    for position, row in enumerate(rows):
        block = jnp.where(index == position, row, block)
    return block


def three_parts(block):
    first = block.astype(half).astype(full)
    rest = block - first
    second = rest.astype(half).astype(full)
    return first, second, rest - second


def source_features(x, y, z):
    norm = x * x + y * y + z * z
    a, b, c = three_parts(rows_of((8, x.shape[1]), (x, y, z, norm, 1.0)))
    return jnp.concatenate([a, b, a, b, c, a], axis=0).T.astype(half)


def target_features(x, y, z):
    norm = x * x + y * y + z * z + soften
    a, b, c = three_parts(rows_of((8, x.shape[1]), (-2.0 * x, -2.0 * y, -2.0 * z, 1.0, norm)))
    return jnp.concatenate([a, a, b, b, a, c], axis=0).astype(half)


def two_parts(block):
    first = block.astype(half)
    return first, (block - first.astype(full)).astype(half)


def split_weights(block):
    first = block.astype(half).astype(full)
    return jnp.concatenate([first, block - first], axis=0).astype(half)


def product(left, right):
    return jnp.dot(left, right, preferred_element_type=full)


def weighted_sum(values, weights):
    high, low = two_parts(values)
    both = product(
        jnp.concatenate([weights, weights], axis=1), jnp.concatenate([high, low], axis=0)
    )
    return both[:8] + both[8:]


def influence_sum(targets, sources, weights):
    return weighted_sum(lax.rsqrt(product(sources, targets)), weights)


def point_row(bodies, member, axis):
    return 8 * bodies + 3 * member + axis


def surface_row(bodies, entry):
    return 11 * bodies + entry


def tile_rows(bodies):
    return -(-(11 * bodies + 3) // 8) * 8


def body_points(tile, bodies, member):
    return [
        tile[point_row(bodies, member, axis) : point_row(bodies, member, axis) + 1, :]
        for axis in range(3)
    ]


def surface_points(tile, bodies):
    x, y, weight = [
        tile[surface_row(bodies, entry) : surface_row(bodies, entry) + 1, :] for entry in range(3)
    ]
    return x, y, jnp.full_like(x, -mid_depth), weight


def pack_kernel(base_ref, panels_ref, surface_ref, tile_ref):
    bodies = panels_ref.shape[1]
    base = base_ref[0]
    tile_ref[...] = jnp.zeros_like(tile_ref)
    area = panels_ref[3]
    for member in range(bodies):
        for entry in range(8):
            tile_ref[8 * member + entry : 8 * member + entry + 1, :] = (
                panels_ref[4 + entry, member : member + 1, :] * area[member : member + 1, :]
            )
        centre = (2 * (base + member)).astype(full)
        for axis, shift in enumerate((centre, 0.0, mid_depth)):
            row = point_row(bodies, member, axis)
            tile_ref[row : row + 1, :] = panels_ref[axis, member : member + 1, :] - shift
    group_centre = (2 * base + (bodies - 1)).astype(full)
    row = surface_row(bodies, 0)
    tile_ref[row : row + 1, :] = surface_ref[0:1, :] - group_centre
    tile_ref[row + 1 : row + 2, :] = surface_ref[1:2, :]
    tile_ref[row + 2 : row + 3, :] = surface_ref[2:3, :] * surface_ref[3:4, :]


def prepare_bodies(tile, bodies, columns, features, weights, offset=0):
    for member in range(bodies):
        features[offset + member, columns, :] = source_features(*body_points(tile, bodies, member))
        weights[offset + member, :, columns] = split_weights(tile[8 * member : 8 * member + 8, :])


def prepare_surface(tile, bodies, columns, features, weights, slot):
    x, y, z, weight = surface_points(tile, bodies)
    features[slot, columns, :] = source_features(x, y, z)
    weights[slot, :, columns] = split_weights(rows_of((8, x.shape[1]), (weight,)))


def own_tile_kernel(bodies, tile_ref, acc_ref, features, weights):
    width = tile_ref.shape[1]
    tile = tile_ref[...]
    columns = pl.ds(0, width)
    prepare_bodies(tile, bodies, columns, features, weights)
    prepare_surface(tile, bodies, columns, features, weights, bodies)
    for member in range(bodies):
        x, y, z = body_points(tile, bodies, member)
        self_part = influence_sum(target_features(x, y, z), features[member], weights[member])
        shift = float(2 * member - bodies + 1)
        surface_part = influence_sum(
            target_features(x + shift, y, z), features[bodies], weights[bodies]
        )
        acc_ref[member] = self_part + surface_part


def group_kernel(bodies, base_ref, pairs_ref, tiles_ref, given_ref, acc_ref, features, weights, points):
    count, _, width = tiles_ref.shape
    base = base_ref[0]
    for index in range(count):
        tile = tiles_ref[index]
        columns = pl.ds(index * width, width)
        prepare_bodies(tile, bodies, columns, features, weights)
        prepare_surface(tile, bodies, columns, features, weights, bodies)
    own = tiles_ref[0]
    for member in range(bodies):
        points[member] = rows_of((8, width), body_points(own, bodies, member))
    acc_ref[...] = given_ref[...]

    def targets_of(member, shift):
        block = points[member]
        return target_features(block[0:1] + shift, block[1:2], block[2:3])

    def own_step(step, carry):
        member = step // 2
        on_surface = step % 2
        source = jnp.where(on_surface == 1, bodies, member)
        shift = jnp.where(on_surface == 1, 2 * member - bodies + 1, 0).astype(full)
        acc_ref[member] += influence_sum(
            targets_of(member, shift), features[source, width:, :], weights[source, :, width:]
        )
        return carry

    lax.fori_loop(0, 2 * bodies, own_step, 0)

    def pair_step(step, carry):
        target = pairs_ref[step // 2, step % 2] - base
        source = pairs_ref[step // 2, 1 - step % 2] - base
        inside = (target >= 0) & (target < bodies) & (source >= 0) & (source < bodies)

        @pl.when(inside)
        def _():
            shift = (2 * (target - source)).astype(full)
            acc_ref[target] += influence_sum(
                targets_of(target, shift), features[source], weights[source]
            )

        return carry

    lax.fori_loop(0, 2 * pairs_ref.shape[0], pair_step, 0)


def crossing_kernel(
    bodies, base_ref, pairs_ref, lower_ref, upper_ref, tile_ref, panels_ref, normals_ref, given_ref,
    acc_ref, force_ref, features, weights, points,
):
    count, _, width = lower_ref.shape
    base = base_ref[0]
    for index in range(count):
        columns = pl.ds(index * width, width)
        prepare_bodies(lower_ref[index], bodies, columns, features, weights)
        prepare_bodies(upper_ref[index], bodies, columns, features, weights, bodies)
    own = tile_ref[...]
    for member in range(bodies):
        points[member] = rows_of((8, width), body_points(own, bodies, member))
    acc_ref[...] = given_ref[...]

    def pair_step(step, carry):
        target = pairs_ref[step // 2, step % 2] - base
        source = pairs_ref[step // 2, 1 - step % 2] - base
        crossing = (target >= 0) & (target < bodies) & ((source < 0) | (source >= bodies))

        @pl.when(crossing)
        def _():
            shift = (2 * (target - source)).astype(full)
            slot = jnp.where(source < 0, source + bodies, source)
            block = points[target]
            acc_ref[target] += influence_sum(
                target_features(block[0:1] + shift, block[1:2], block[2:3]),
                features[slot],
                weights[slot],
            )

        return carry

    lax.fori_loop(0, 2 * pairs_ref.shape[0], pair_step, 0)
    lane = lax.broadcasted_iota(jnp.int32, (8, 128), 1)
    for member in range(bodies):
        potential = acc_ref[member]
        area = panels_ref[3, member : member + 1, :]
        out = jnp.zeros((8, 128), full)
        for axis in range(3):
            term = potential * (normals_ref[axis, member : member + 1, :] * area)
            out = jnp.where(lane == axis, jnp.sum(term, axis=1, keepdims=True), out)
        force_ref[member] = out


def velocity_kernel(bodies, tiles_ref, state_ref, next_ref, features, weights):
    count, _, width = tiles_ref.shape
    for index in range(count):
        tile = tiles_ref[index]
        columns = pl.ds(index * width, width)
        for member in range(bodies):
            x, y, z = body_points(tile, bodies, member)
            features[member, columns, :] = source_features(x, y, z)
            first = tile[8 * member : 8 * member + 1, :]
            weights[member, :, columns] = split_weights(
                rows_of((8, width), (first, first * x, first * y, first * z))
            )
    own = tiles_ref[0]
    x, y, z, _ = surface_points(own, bodies)

    def body_step(member, velocity):
        place = x + (bodies - 1 - 2 * member).astype(full)
        inverse = lax.rsqrt(product(features[member], target_features(place, y, z)))
        moments = weighted_sum(inverse * inverse * inverse, weights[member])
        return tuple(
            so_far + (moments[axis + 1 : axis + 2] - at * moments[0:1])
            for axis, (so_far, at) in enumerate(zip(velocity, (place, y, z)))
        )

    zero = jnp.zeros((1, width), full)
    velocity = lax.fori_loop(0, bodies, body_step, (zero, zero, zero))
    speed_sq = velocity[0] * velocity[0] + velocity[1] * velocity[1] + velocity[2] * velocity[2]
    potential, elevation = state_ref[0:1, :], state_ref[1:2, :]
    next_ref[0:1, :] = potential + time_step * (-gravity * elevation - 0.5 * speed_sq)
    next_ref[1:2, :] = elevation + time_step * velocity[2]


def call(kernel, out_shapes, operands, scalars=0, scratch=(), units=0.0):
    specs = [pl.BlockSpec(memory_space=pltpu.SMEM)] * scalars
    specs += [pl.BlockSpec(memory_space=pltpu.VMEM)] * (len(operands) - scalars)
    several = isinstance(out_shapes, list)
    shapes = [jax.ShapeDtypeStruct(shape, full) for shape in (out_shapes if several else [out_shapes])]
    result = pl.pallas_call(
        kernel,
        out_shape=shapes,
        in_specs=specs,
        out_specs=[pl.BlockSpec(memory_space=pltpu.VMEM)] * len(shapes),
        scratch_shapes=list(scratch),
        compiler_params=pltpu.CompilerParams(vmem_limit_bytes=48 * 1024 * 1024),
        cost_estimate=pl.CostEstimate(
            flops=int(units * 1.2e9), bytes_accessed=1024, transcendentals=0
        ),
    )(*operands)
    return result if several else result[0]


def rotations(block, axis):
    count = lax.axis_size(axis)
    return [
        lax.ppermute(block, axis, [(i, (i + k) % count) for i in range(count)])
        for k in range(1, count)
    ]


def on_device(body_panels, body_normals, fs_panels, fs_state, pairs):
    bodies = body_panels.shape[1]
    width = body_panels.shape[2]
    tiles_count = lax.axis_size("surf")
    groups = lax.axis_size("body")
    base = (lax.axis_index("body") * bodies).astype(jnp.int32).reshape(1)
    own = call(
        pack_kernel, (tile_rows(bodies), width), (base, body_panels, fs_panels), scalars=1
    )
    if tiles_count == 4:
        tiles = jnp.stack([own] + rotations(own, "surf"))
    else:
        everything = lax.all_gather(own, "surf")
        tiles = jnp.concatenate(
            [own[None]]
            + [
                lax.dynamic_index_in_dim(
                    everything, (lax.axis_index("surf") + k) % tiles_count, 0
                )
                for k in range(1, tiles_count)
            ]
        )
    wide = width * tiles_count
    acc_shape = (bodies, 8, width)
    partial = call(
        functools.partial(own_tile_kernel, bodies),
        acc_shape,
        (own,),
        scratch=(
            pltpu.VMEM((bodies + 1, width, DEPTH), half),
            pltpu.VMEM((bodies + 1, 16, width), half),
        ),
        units=2.0,
    )
    lower = lax.ppermute(tiles, "body", [(i, i + 1) for i in range(groups - 1)])
    upper = lax.ppermute(tiles, "body", [(i + 1, i) for i in range(groups - 1)])
    points = pltpu.VMEM((bodies, 8, width), full)
    partial = call(
        functools.partial(group_kernel, bodies),
        acc_shape,
        (base, pairs, tiles, partial),
        scalars=2,
        scratch=(
            pltpu.VMEM((bodies + 1, wide, DEPTH), half),
            pltpu.VMEM((bodies + 1, 16, wide), half),
            points,
        ),
        units=7.0,
    )
    own_potential, force = call(
        functools.partial(crossing_kernel, bodies),
        [acc_shape, (bodies, 8, 128)],
        (base, pairs, lower, upper, own, body_panels, body_normals, partial),
        scalars=2,
        scratch=(
            pltpu.VMEM((2 * bodies, wide, DEPTH), half),
            pltpu.VMEM((2 * bodies, 16, wide), half),
            points,
        ),
        units=6.0,
    )
    fs_next = call(
        functools.partial(velocity_kernel, bodies),
        (2, width),
        (tiles, fs_state),
        scratch=(
            pltpu.VMEM((bodies, wide, DEPTH), half),
            pltpu.VMEM((bodies, 16, wide), half),
        ),
        units=5.0,
    )
    if tiles_count == 4:
        first, second, third = rotations(force, "surf")
        total = (force + second) + (first + third)
    else:
        total = lax.psum(force, "surf")
    return own_potential, total[:, :, :3], fs_next


def solution(mesh):
    placed = (
        P(None, "body", "surf"),
        P(None, "body", "surf"),
        P(None, ("body", "surf")),
        P(None, ("body", "surf")),
        P(),
    )
    return jax.shard_map(
        on_device,
        mesh=mesh,
        in_specs=placed,
        out_specs=(P("body", None, "surf"), P("body", None, None), P(None, ("body", "surf"))),
        check_vma=False,
    )
```

```python
import functools

import jax
import jax.numpy as jnp
from jax import lax
from jax.experimental import pallas as pl
from jax.experimental.pallas import tpu as pltpu
from jax.sharding import PartitionSpec as P

soften = 0.01
gravity = 9.81
time_step = 0.2
mid_depth = -1.5
half = jnp.bfloat16
full = jnp.float32
DEPTH = 48


def rows_of(block_shape, rows):
    index = lax.broadcasted_iota(jnp.int32, block_shape, 0)
    block = jnp.zeros(block_shape, full)
    for position, row in enumerate(rows):
        block = jnp.where(index == position, row, block)
    return block


def three_parts(block):
    first = block.astype(half).astype(full)
    rest = block - first
    second = rest.astype(half).astype(full)
    return first, second, rest - second


def source_features(x, y, z):
    norm = x * x + y * y + z * z
    a, b, c = three_parts(rows_of((8, x.shape[1]), (x, y, z, norm, 1.0)))
    return jnp.concatenate([a, b, a, b, c, a], axis=0).T.astype(half)


def target_features(x, y, z):
    norm = x * x + y * y + z * z + soften
    a, b, c = three_parts(rows_of((8, x.shape[1]), (-2.0 * x, -2.0 * y, -2.0 * z, 1.0, norm)))
    return jnp.concatenate([a, a, b, b, a, c], axis=0).astype(half)


def two_parts(block):
    first = block.astype(half)
    return first, (block - first.astype(full)).astype(half)


def split_weights(block):
    first = block.astype(half).astype(full)
    return jnp.concatenate([first, block - first], axis=0).astype(half)


def product(left, right):
    return jnp.dot(left, right, preferred_element_type=full)


def weighted_sum(values, weights):
    high, low = two_parts(values)
    both = product(
        jnp.concatenate([weights, weights], axis=1), jnp.concatenate([high, low], axis=0)
    )
    return both[:8] + both[8:]


def influence_sum(targets, sources, weights):
    return weighted_sum(lax.rsqrt(product(sources, targets)), weights)


def point_row(bodies, member, axis):
    return 8 * bodies + 3 * member + axis


def surface_row(bodies, entry):
    return 11 * bodies + entry


def tile_rows(bodies):
    return -(-(11 * bodies + 3) // 8) * 8


def body_points(tile, bodies, member):
    return [
        tile[point_row(bodies, member, axis) : point_row(bodies, member, axis) + 1, :]
        for axis in range(3)
    ]


def surface_points(tile, bodies):
    x, y, weight = [
        tile[surface_row(bodies, entry) : surface_row(bodies, entry) + 1, :] for entry in range(3)
    ]
    return x, y, jnp.full_like(x, -mid_depth), weight


def pack_kernel(panels_hbm, surface_hbm, tile_ref, panels_ref, surface_ref, sems):
    bodies = panels_ref.shape[1]
    copies = [
        pltpu.make_async_copy(panels_hbm, panels_ref, sems.at[0]),
        pltpu.make_async_copy(surface_hbm, surface_ref, sems.at[1]),
    ]
    for copy in copies:
        copy.start()
    base = lax.axis_index("body") * bodies
    tile_ref[...] = jnp.zeros_like(tile_ref)
    for copy in copies:
        copy.wait()
    area = panels_ref[3]
    for member in range(bodies):
        for entry in range(8):
            tile_ref[8 * member + entry : 8 * member + entry + 1, :] = (
                panels_ref[4 + entry, member : member + 1, :] * area[member : member + 1, :]
            )
        centre = (2 * (base + member)).astype(full)
        for axis, shift in enumerate((centre, 0.0, mid_depth)):
            row = point_row(bodies, member, axis)
            tile_ref[row : row + 1, :] = panels_ref[axis, member : member + 1, :] - shift
    group_centre = (2 * base + (bodies - 1)).astype(full)
    row = surface_row(bodies, 0)
    tile_ref[row : row + 1, :] = surface_ref[0:1, :] - group_centre
    tile_ref[row + 1 : row + 2, :] = surface_ref[1:2, :]
    tile_ref[row + 2 : row + 3, :] = surface_ref[2:3, :] * surface_ref[3:4, :]


def body_weights(tile, member):
    return split_weights(tile[8 * member : 8 * member + 8, :])


def moment_weights(tile, bodies, member):
    x, y, z = body_points(tile, bodies, member)
    first = tile[8 * member : 8 * member + 1, :]
    return split_weights(rows_of((8, x.shape[1]), (first, first * x, first * y, first * z)))


def prepare_tile(tile, bodies, columns, features, weights, spread):
    for member in range(bodies):
        features[member, columns, :] = source_features(*body_points(tile, bodies, member))
        weights[member, :, columns] = body_weights(tile, member)
    x, y, z, weight = surface_points(tile, bodies)
    features[bodies, columns, :] = source_features(x, y, z)
    spread[columns, :] = jnp.broadcast_to(weight, (128, x.shape[1])).T


def surface_sum(targets, sources, spread):
    values = lax.rsqrt(product(sources, targets))
    count, width = values.shape
    sums = []
    for start in range(0, width, 128):
        term = values[:, start : start + 128] * spread
        sums.append(jnp.sum(term.reshape(count // 8, 8, 128), axis=0))
    return jnp.sum(jnp.concatenate(sums, axis=1), axis=0, keepdims=True)


def velocity_term(features, weights, place, y, z):
    inverse = lax.rsqrt(product(features, target_features(place, y, z)))
    moments = weighted_sum(inverse * inverse * inverse, weights)
    return [
        moments[axis + 1 : axis + 2] - at * moments[0:1] for axis, at in enumerate((place, y, z))
    ]


def targets_of(points, member, shift):
    block = points[member]
    return target_features(block[0:1] + shift, block[1:2], block[2:3])


def group_sums(bodies, edges, inner, points, features, weights, spread, acc_ref):
    def own_step(member, carry):
        acc_ref[member] += influence_sum(
            targets_of(points, member, 0.0), features[member], weights[member]
        )
        shift = (2 * member - (bodies - 1)).astype(full)
        acc_ref[member, 0:1, :] += surface_sum(
            targets_of(points, member, shift), features[bodies], spread[...]
        )
        return carry

    lax.fori_loop(0, bodies, own_step, 0)
    inner()

    def pair_step(step, carry):
        target, source = edges[0, step], edges[1, step]
        shift = (2 * (target - source)).astype(full)
        acc_ref[target] += influence_sum(
            targets_of(points, target, shift), features[source], weights[source]
        )
        return carry

    lax.fori_loop(0, edges[4, 0], pair_step, 0)


def own_tile_kernel(
    bodies, pairs_hbm, tile_ref, acc_ref, velocity_ref, edges,
    features, weights, spread, points, pairs, sem,
):
    width = tile_ref.shape[1]
    copy = pltpu.make_async_copy(pairs_hbm, pairs, sem)
    copy.start()
    tile = tile_ref[...]
    prepare_tile(tile, bodies, pl.ds(0, width), features, weights, spread)
    for member in range(bodies):
        points[member] = rows_of((8, width), body_points(tile, bodies, member))
    acc_ref[...] = jnp.zeros_like(acc_ref)
    base = lax.axis_index("body") * bodies

    def list_edges():
        copy.wait()
        for slot in range(2 + 2 * bodies):
            edges[4, slot] = 0

        def step_edge(step, carry):
            target = pairs[step % 2, step // 2] - base
            source = pairs[1 - step % 2, step // 2] - base

            @pl.when((target >= 0) & (target < bodies))
            def _():
                inside = (source >= 0) & (source < bodies)
                row = jnp.where(inside, 0, 1)
                place = edges[4, row]
                edges[2 * row, place] = target
                edges[2 * row + 1, place] = source
                edges[4, row] = place + 1

                @pl.when(jnp.logical_not(inside))
                def _():
                    edges[4, 2 + jnp.where(source < 0, source + bodies, source)] = 1

            return carry

        lax.fori_loop(0, 2 * pairs.shape[1], step_edge, 0)

    group_sums(bodies, edges, list_edges, points, features, weights, spread, acc_ref)
    x, y, z, _ = surface_points(tile, bodies)
    total = [jnp.zeros((1, width), full)] * 3
    for member in range(bodies):
        term = velocity_term(
            features[member], moment_weights(tile, bodies, member), x + float(bodies - 1 - 2 * member), y, z
        )
        total = [so_far + part for so_far, part in zip(total, term)]
    velocity_ref[...] = rows_of((8, width), total)


def group_kernel(
    bodies, edges_hbm, tiles_ref, given_ref, acc_ref, features, weights, spread, points, edges, sem
):
    count, _, width = tiles_ref.shape
    copy = pltpu.make_async_copy(edges_hbm, edges, sem)
    copy.start()
    for index in range(1, count):
        columns = pl.ds((index - 1) * width, width)
        prepare_tile(tiles_ref[index], bodies, columns, features, weights, spread)
    own = tiles_ref[0]
    for member in range(bodies):
        points[member] = rows_of((8, width), body_points(own, bodies, member))
    acc_ref[...] = given_ref[...]
    group_sums(bodies, edges, copy.wait, points, features, weights, spread, acc_ref)


def crossing_kernel(
    bodies, edges_hbm, lower_ref, upper_ref, tile_ref, panels_ref, normals_ref, given_ref,
    potential_hbm, force_ref, acc_ref, features, weights, points, edges, sems,
):
    count, _, width = lower_ref.shape
    copy = pltpu.make_async_copy(edges_hbm, edges, sems.at[0])
    copy.start()
    own = tile_ref[...]
    for member in range(bodies):
        points[member] = rows_of((8, width), body_points(own, bodies, member))
    acc_ref[...] = given_ref[...]
    force_ref[...] = jnp.zeros_like(force_ref)
    copy.wait()
    for slot in range(2 * bodies):

        @pl.when(edges[4, 2 + slot] == 1)
        def _():
            side = lower_ref if slot < bodies else upper_ref
            for index in range(count):
                columns = pl.ds(index * width, width)
                tile = side[index]
                member = slot % bodies
                features[slot, columns, :] = source_features(*body_points(tile, bodies, member))
                weights[slot, :, columns] = body_weights(tile, member)

    def pair_step(step, carry):
        target, source = edges[2, step], edges[3, step]
        shift = (2 * (target - source)).astype(full)
        slot = jnp.where(source < 0, source + bodies, source)
        acc_ref[target] += influence_sum(
            targets_of(points, target, shift), features[slot], weights[slot]
        )
        return carry

    lax.fori_loop(0, edges[4, 1], pair_step, 0)
    store = pltpu.make_async_copy(acc_ref, potential_hbm, sems.at[1])
    store.start()
    for member in range(bodies):
        area = panels_ref[3, member : member + 1, :]
        scaled = rows_of(
            (8, width), [normals_ref[axis, member : member + 1, :] * area for axis in range(3)]
        )
        force_ref[member, :, 0:8] = lax.dot_general(
            scaled,
            acc_ref[member],
            (((1,), (1,)), ((), ())),
            precision=lax.Precision.HIGHEST,
            preferred_element_type=full,
        )
    store.wait()


def velocity_kernel(bodies, tiles_ref, features, given_ref, state_ref, next_ref, weights):
    count, _, width = tiles_ref.shape
    for index in range(1, count):
        tile = tiles_ref[index]
        for member in range(bodies):
            weights[member, :, pl.ds((index - 1) * width, width)] = moment_weights(
                tile, bodies, member
            )
    own = tiles_ref[0]
    x, y, z, _ = surface_points(own, bodies)

    def body_step(member, velocity):
        place = x + (bodies - 1 - 2 * member).astype(full)
        term = velocity_term(features[member], weights[member], place, y, z)
        return tuple(so_far + part for so_far, part in zip(velocity, term))

    start = tuple(given_ref[axis : axis + 1, :] for axis in range(3))
    velocity = lax.fori_loop(0, bodies, body_step, start)
    speed_sq = velocity[0] * velocity[0] + velocity[1] * velocity[1] + velocity[2] * velocity[2]
    potential, elevation = state_ref[0:1, :], state_ref[1:2, :]
    next_ref[0:1, :] = potential + time_step * (-gravity * elevation - 0.5 * speed_sq)
    next_ref[1:2, :] = elevation + time_step * velocity[2]


VMEM, SMEM, ANY = pltpu.VMEM, pltpu.SMEM, pl.ANY


def call(kernel, operands, results, scratch=(), units=0.0):
    single = len(results) == 1
    out = pl.pallas_call(
        kernel,
        out_shape=[jax.ShapeDtypeStruct(shape, kind) for _, shape, kind in results],
        in_specs=[pl.BlockSpec(memory_space=space) for space, _ in operands],
        out_specs=[pl.BlockSpec(memory_space=space) for space, _, _ in results],
        scratch_shapes=list(scratch),
        compiler_params=pltpu.CompilerParams(vmem_limit_bytes=40 * 1024 * 1024),
        cost_estimate=pl.CostEstimate(
            flops=int(units * 1.2e9), bytes_accessed=1024, transcendentals=0
        ),
    )(*[array for _, array in operands])
    return out[0] if single else out


def rotations(block, axis):
    count = lax.axis_size(axis)
    return [
        lax.ppermute(block, axis, [(i, (i + k) % count) for i in range(count)])
        for k in range(1, count)
    ]


def on_device(body_panels, body_normals, fs_panels, fs_state, pairs):
    bodies = body_panels.shape[1]
    width = body_panels.shape[2]
    tiles_count = lax.axis_size("surf")
    groups = lax.axis_size("body")
    semaphore = pltpu.SemaphoreType.DMA
    own = call(
        pack_kernel,
        [(ANY, body_panels), (ANY, fs_panels)],
        [(VMEM, (tile_rows(bodies), width), full)],
        scratch=(VMEM(body_panels.shape, full), VMEM(fs_panels.shape, full), semaphore((2,))),
    )
    if tiles_count == 4:
        tiles = jnp.stack([own] + rotations(own, "surf"))
    else:
        everything = lax.all_gather(own, "surf")
        tiles = jnp.concatenate(
            [own[None]]
            + [
                lax.dynamic_index_in_dim(
                    everything, (lax.axis_index("surf") + k) % tiles_count, 0
                )
                for k in range(1, tiles_count)
            ]
        )
    wide = width * tiles_count
    rest = wide - width
    acc_shape = (bodies, 8, width)
    edges_shape = (5, max(2 * pairs.shape[0], 2 + 2 * bodies))
    points = VMEM(acc_shape, full)
    edges_space = SMEM(edges_shape, jnp.int32)
    partial, velocity, edges = call(
        functools.partial(own_tile_kernel, bodies),
        [(ANY, pairs.T), (VMEM, own)],
        [
            (VMEM, acc_shape, full),
            (VMEM, (8, width), full),
            (SMEM, edges_shape, jnp.int32),
        ],
        scratch=(
            VMEM((bodies + 1, width, DEPTH), half),
            VMEM((bodies, 16, width), half),
            VMEM((width, 128), full),
            points,
            SMEM((2, pairs.shape[0]), jnp.int32),
            semaphore,
        ),
        units=3.0,
    )
    lower = lax.ppermute(tiles, "body", [(i, i + 1) for i in range(groups - 1)])
    upper = lax.ppermute(tiles, "body", [(i + 1, i) for i in range(groups - 1)])
    partial, features = call(
        functools.partial(group_kernel, bodies),
        [(ANY, edges), (VMEM, tiles), (VMEM, partial)],
        [(VMEM, acc_shape, full), (VMEM, (bodies + 1, rest, DEPTH), half)],
        scratch=(
            VMEM((bodies, 16, rest), half),
            VMEM((rest, 128), full),
            points,
            edges_space,
            semaphore,
        ),
        units=7.0,
    )
    own_potential, force = call(
        functools.partial(crossing_kernel, bodies),
        [(ANY, edges), (VMEM, lower), (VMEM, upper), (VMEM, own), (VMEM, body_panels),
         (VMEM, body_normals), (VMEM, partial)],
        [(ANY, acc_shape, full), (VMEM, (bodies, 8, 128), full)],
        scratch=(
            VMEM(acc_shape, full),
            VMEM((2 * bodies, wide, DEPTH), half),
            VMEM((2 * bodies, 16, wide), half),
            points,
            edges_space,
            semaphore((2,)),
        ),
        units=6.0,
    )
    fs_next = call(
        functools.partial(velocity_kernel, bodies),
        [(VMEM, tiles), (VMEM, features), (VMEM, velocity), (VMEM, fs_state)],
        [(VMEM, (2, width), full)],
        scratch=(VMEM((bodies, 16, rest), half),),
        units=5.0,
    )
    if tiles_count == 4:
        first, second, third = rotations(force, "surf")
        total = (force + second) + (first + third)
    else:
        total = lax.psum(force, "surf")
    return own_potential, total[:, :3, :8].transpose(0, 2, 1), fs_next


def solution(mesh):
    placed = (
        P(None, "body", "surf"),
        P(None, "body", "surf"),
        P(None, ("body", "surf")),
        P(None, ("body", "surf")),
        P(),
    )
    return jax.shard_map(
        on_device,
        mesh=mesh,
        in_specs=placed,
        out_specs=(P("body", None, "surf"), P("body", None, None), P(None, ("body", "surf"))),
        check_vma=False,
    )
```

```python
import functools

import jax
import jax.numpy as jnp
from jax import lax
from jax.experimental import pallas as pl
from jax.experimental.pallas import tpu as pltpu
from jax.sharding import PartitionSpec as P

soften = 0.01
gravity = 9.81
time_step = 0.2
mid_depth = -1.5
half = jnp.bfloat16
full = jnp.float32
DEPTH = 48


def rows_of(block_shape, rows):
    index = lax.broadcasted_iota(jnp.int32, block_shape, 0)
    block = jnp.zeros(block_shape, full)
    for position, row in enumerate(rows):
        block = jnp.where(index == position, row, block)
    return block


def three_parts(block):
    first = block.astype(half).astype(full)
    rest = block - first
    second = rest.astype(half).astype(full)
    return first, second, rest - second


def source_features(x, y, z):
    norm = x * x + y * y + z * z
    a, b, c = three_parts(rows_of((8, x.shape[1]), (x, y, z, norm, 1.0)))
    return jnp.concatenate([a, b, a, b, c, a], axis=0).T.astype(half)


def target_features(x, y, z):
    norm = x * x + y * y + z * z + soften
    a, b, c = three_parts(rows_of((8, x.shape[1]), (-2.0 * x, -2.0 * y, -2.0 * z, 1.0, norm)))
    return jnp.concatenate([a, a, b, b, a, c], axis=0).astype(half)


def two_parts(block):
    first = block.astype(half)
    return first, (block - first.astype(full)).astype(half)


def split_weights(block):
    first = block.astype(half).astype(full)
    return jnp.concatenate([first, block - first], axis=0).astype(half)


def product(left, right):
    return jnp.dot(left, right, preferred_element_type=full)


def weighted_sum(values, weights):
    high, low = two_parts(values)
    both = product(
        jnp.concatenate([weights, weights], axis=1), jnp.concatenate([high, low], axis=0)
    )
    return both[:8] + both[8:]


def influence_sum(targets, sources, weights):
    return weighted_sum(lax.rsqrt(product(sources, targets)), weights)


def point_row(bodies, member, axis):
    return 8 * bodies + 3 * member + axis


def surface_row(bodies, entry):
    return 11 * bodies + entry


def tile_rows(bodies):
    return -(-(11 * bodies + 3) // 8) * 8


def body_points(tile, bodies, member):
    return [
        tile[point_row(bodies, member, axis) : point_row(bodies, member, axis) + 1, :]
        for axis in range(3)
    ]


def surface_points(tile, bodies):
    x, y, weight = [
        tile[surface_row(bodies, entry) : surface_row(bodies, entry) + 1, :] for entry in range(3)
    ]
    return x, y, jnp.full_like(x, -mid_depth), weight


def pack_kernel(panels_hbm, surface_hbm, tile_ref, panels_ref, surface_ref, sems):
    bodies = panels_ref.shape[1]
    copies = [
        pltpu.make_async_copy(panels_hbm, panels_ref, sems.at[0]),
        pltpu.make_async_copy(surface_hbm, surface_ref, sems.at[1]),
    ]
    for copy in copies:
        copy.start()
    base = lax.axis_index("body") * bodies
    tile_ref[...] = jnp.zeros_like(tile_ref)
    for copy in copies:
        copy.wait()
    area = panels_ref[3]
    for member in range(bodies):
        for entry in range(8):
            tile_ref[8 * member + entry : 8 * member + entry + 1, :] = (
                panels_ref[4 + entry, member : member + 1, :] * area[member : member + 1, :]
            )
        centre = (2 * (base + member)).astype(full)
        for axis, shift in enumerate((centre, 0.0, mid_depth)):
            row = point_row(bodies, member, axis)
            tile_ref[row : row + 1, :] = panels_ref[axis, member : member + 1, :] - shift
    group_centre = (2 * base + (bodies - 1)).astype(full)
    row = surface_row(bodies, 0)
    tile_ref[row : row + 1, :] = surface_ref[0:1, :] - group_centre
    tile_ref[row + 1 : row + 2, :] = surface_ref[1:2, :]
    tile_ref[row + 2 : row + 3, :] = surface_ref[2:3, :] * surface_ref[3:4, :]


def body_weights(tile, member):
    return split_weights(tile[8 * member : 8 * member + 8, :])


def moment_weights(tile, bodies, member):
    x, y, z = body_points(tile, bodies, member)
    first = tile[8 * member : 8 * member + 1, :]
    return split_weights(rows_of((8, x.shape[1]), (first, first * x, first * y, first * z)))


def prepare_tile(tile, bodies, columns, features, weights, spread):
    for member in range(bodies):
        features[member, columns, :] = source_features(*body_points(tile, bodies, member))
        weights[member, :, columns] = body_weights(tile, member)
    x, y, z, weight = surface_points(tile, bodies)
    features[bodies, columns, :] = source_features(x, y, z)
    spread[columns, :] = jnp.broadcast_to(weight, (128, x.shape[1])).T


def surface_sum(targets, sources, spread):
    values = lax.rsqrt(product(sources, targets))
    count, width = values.shape
    sums = []
    for start in range(0, width, 128):
        term = values[:, start : start + 128] * spread
        sums.append(jnp.sum(term.reshape(count // 8, 8, 128), axis=0))
    return jnp.sum(jnp.concatenate(sums, axis=1), axis=0, keepdims=True)


def velocity_term(features, weights, place, y, z):
    inverse = lax.rsqrt(product(features, target_features(place, y, z)))
    moments = weighted_sum(inverse * inverse * inverse, weights)
    return [
        moments[axis + 1 : axis + 2] - at * moments[0:1] for axis, at in enumerate((place, y, z))
    ]


def targets_of(points, member, shift):
    block = points[member]
    return target_features(block[0:1] + shift, block[1:2], block[2:3])


def code_rows(pair_count):
    return 4 * pair_count + 1


def own_tile_kernel(
    bodies, pairs_hbm, tile_ref, acc_ref, velocity_ref, features, codes,
    weights, spread, pairs, counts, sem,
):
    width = tile_ref.shape[1]
    copy = pltpu.make_async_copy(pairs_hbm, pairs, sem)
    copy.start()
    tile = tile_ref[...]
    prepare_tile(tile, bodies, pl.ds(0, width), features, weights, spread)
    x, y, z, _ = surface_points(tile, bodies)
    total = [jnp.zeros((1, width), full)] * 3
    index = lax.broadcasted_iota(jnp.int32, (8, width), 0)
    for member in range(bodies):
        point = body_points(tile, bodies, member)
        self_part = influence_sum(target_features(*point), features[member], weights[member])
        shift = float(2 * member - (bodies - 1))
        surface_part = surface_sum(
            target_features(point[0] + shift, point[1], point[2]), features[bodies], spread[...]
        )
        acc_ref[member] = self_part + jnp.where(index == 0, surface_part, 0.0)
        term = velocity_term(
            features[member], moment_weights(tile, bodies, member), x - shift, y, z
        )
        total = [so_far + part for so_far, part in zip(total, term)]
    velocity_ref[...] = rows_of((8, width), total)

    base = lax.axis_index("body") * bodies
    pair_count = pairs.shape[1]
    copy.wait()
    for entry in range(3):
        counts[entry] = 0

    def step_edge(step, carry):
        target = pairs[step % 2, step // 2] - base
        source = pairs[1 - step % 2, step // 2] - base

        @pl.when((target >= 0) & (target < bodies))
        def _():
            inside = (source >= 0) & (source < bodies)
            row = jnp.where(inside, 0, 1)
            slot = jnp.where(source < 0, source + bodies, source)
            place = counts[row]
            codes[pl.ds(row * 2 * pair_count + place, 1), :] = jnp.full(
                (1, 128), target * 16 + slot, jnp.int32
            )
            counts[row] = place + 1
            counts[2] = counts[2] | jnp.where(inside, 0, jnp.left_shift(1, slot))

        return carry

    lax.fori_loop(0, 2 * pair_count, step_edge, 0)
    lane = lax.broadcasted_iota(jnp.int32, (1, 128), 1)
    codes[4 * pair_count : 4 * pair_count + 1, :] = jnp.where(
        lane == 0, counts[0], jnp.where(lane == 1, counts[1], counts[2])
    )


def over_codes(codes, first, count, visit):
    def step_code(step, code):
        following = codes[first + step + 1, 0]
        visit(code // 16, code % 16)
        return following

    lax.fori_loop(0, count, step_code, codes[first, 0])


def group_kernel(
    bodies, codes, tiles_ref, given_ref, own_features, acc_ref, features, weights, spread, surface, points
):
    count, _, width = tiles_ref.shape
    rest = (count - 1) * width
    pair_count = codes.shape[0] // 4
    for index in range(1, count):
        tile = tiles_ref[index]
        columns = pl.ds((index - 1) * width, width)
        for member in range(bodies):
            features[member, columns, :] = source_features(*body_points(tile, bodies, member))
            weights[member, :, columns] = body_weights(tile, member)
        x, y, z, weight = surface_points(tile, bodies)
        surface[columns, :] = source_features(x, y, z)
        spread[columns, :] = jnp.broadcast_to(weight, (128, width)).T
    own = tiles_ref[0]
    for member in range(bodies):
        points[member] = rows_of((8, width), body_points(own, bodies, member))
        features[member, rest:, :] = own_features[member]
        weights[member, :, rest:] = body_weights(own, member)

    def own_step(member, carry):
        acc_ref[member] = given_ref[member] + influence_sum(
            targets_of(points, member, 0.0), features[member, :rest, :], weights[member, :, :rest]
        )
        shift = (2 * member - (bodies - 1)).astype(full)
        acc_ref[member, 0:1, :] += surface_sum(
            targets_of(points, member, shift), surface[...], spread[...]
        )
        return carry

    lax.fori_loop(0, bodies, own_step, 0)

    def visit(target, source):
        shift = (2 * (target - source)).astype(full)
        acc_ref[target] += influence_sum(
            targets_of(points, target, shift), features[source], weights[source]
        )

    over_codes(codes, 0, codes[4 * pair_count, 0], visit)


def crossing_kernel(
    bodies, codes, lower_ref, upper_ref, tile_ref, panels_ref, normals_ref, given_ref,
    acc_ref, force_ref, features, weights, points,
):
    count, _, width = lower_ref.shape
    pair_count = codes.shape[0] // 4
    used = codes[4 * pair_count, 2]
    crossings = codes[4 * pair_count, 1]
    own = tile_ref[...]
    for member in range(bodies):
        points[member] = rows_of((8, width), body_points(own, bodies, member))
    acc_ref[...] = given_ref[...]
    force_ref[...] = jnp.zeros_like(force_ref)
    for slot in range(2 * bodies):

        @pl.when((jnp.right_shift(used, slot) & 1) == 1)
        def _():
            side = lower_ref if slot < bodies else upper_ref
            for index in range(count):
                columns = pl.ds(index * width, width)
                tile = side[index]
                member = slot % bodies
                features[slot, columns, :] = source_features(*body_points(tile, bodies, member))
                weights[slot, :, columns] = body_weights(tile, member)

    def visit(target, slot):
        source = jnp.where(slot < bodies, slot - bodies, slot)
        shift = (2 * (target - source)).astype(full)
        acc_ref[target] += influence_sum(
            targets_of(points, target, shift), features[slot], weights[slot]
        )

    over_codes(codes, 2 * pair_count, crossings, visit)
    for member in range(bodies):
        area = panels_ref[3, member : member + 1, :]
        scaled = rows_of(
            (8, width), [normals_ref[axis, member : member + 1, :] * area for axis in range(3)]
        )
        force_ref[member, :, 0:8] = lax.dot_general(
            scaled,
            acc_ref[member],
            (((1,), (1,)), ((), ())),
            precision=lax.Precision.HIGHEST,
            preferred_element_type=full,
        )


def velocity_kernel(
    bodies, tiles_ref, features, given_ref, state_ref, potential_ref, next_ref, potential_hbm, weights, sem
):
    count, _, width = tiles_ref.shape
    rest = (count - 1) * width
    store = pltpu.make_async_copy(potential_ref, potential_hbm, sem)
    store.start()
    for index in range(1, count):
        tile = tiles_ref[index]
        for member in range(bodies):
            weights[member, :, pl.ds((index - 1) * width, width)] = moment_weights(
                tile, bodies, member
            )
    own = tiles_ref[0]
    x, y, z, _ = surface_points(own, bodies)

    def body_step(member, velocity):
        place = x + (bodies - 1 - 2 * member).astype(full)
        term = velocity_term(features[member, :rest, :], weights[member], place, y, z)
        return tuple(so_far + part for so_far, part in zip(velocity, term))

    start = tuple(given_ref[axis : axis + 1, :] for axis in range(3))
    velocity = lax.fori_loop(0, bodies, body_step, start)
    speed_sq = velocity[0] * velocity[0] + velocity[1] * velocity[1] + velocity[2] * velocity[2]
    potential, elevation = state_ref[0:1, :], state_ref[1:2, :]
    next_ref[0:1, :] = potential + time_step * (-gravity * elevation - 0.5 * speed_sq)
    next_ref[1:2, :] = elevation + time_step * velocity[2]
    store.wait()


def finish_kernel(own_ref, first_ref, second_ref, third_ref, next_ref, force_ref, out_ref):
    total = (own_ref[...] + second_ref[...]) + (first_ref[...] + third_ref[...])
    force_ref[...] = total[:, :3, :8]
    out_ref[...] = next_ref[...]


VMEM, SMEM, HBM = pltpu.VMEM, pltpu.SMEM, pltpu.HBM


def call(kernel, operands, results, scratch=(), units=0.0):
    single = len(results) == 1
    out = pl.pallas_call(
        kernel,
        out_shape=[jax.ShapeDtypeStruct(shape, kind) for _, shape, kind in results],
        in_specs=[pl.BlockSpec(memory_space=space) for space, _ in operands],
        out_specs=[pl.BlockSpec(memory_space=space) for space, _, _ in results],
        scratch_shapes=list(scratch),
        compiler_params=pltpu.CompilerParams(vmem_limit_bytes=40 * 1024 * 1024),
        cost_estimate=pl.CostEstimate(
            flops=int(units * 1.2e9), bytes_accessed=1024, transcendentals=0
        ),
    )(*[array for _, array in operands])
    return out[0] if single else out


def rotations(block, axis):
    count = lax.axis_size(axis)
    return [
        lax.ppermute(block, axis, [(i, (i + k) % count) for i in range(count)])
        for k in range(1, count)
    ]


def on_device(body_panels, body_normals, fs_panels, fs_state, pairs):
    bodies = body_panels.shape[1]
    width = body_panels.shape[2]
    tiles_count = lax.axis_size("surf")
    groups = lax.axis_size("body")
    pair_count = pairs.shape[0]
    semaphore = pltpu.SemaphoreType.DMA
    own = call(
        pack_kernel,
        [(HBM, body_panels), (HBM, fs_panels)],
        [(VMEM, (tile_rows(bodies), width), full)],
        scratch=(VMEM(body_panels.shape, full), VMEM(fs_panels.shape, full), semaphore((2,))),
    )
    if tiles_count == 4:
        tiles = jnp.stack([own] + rotations(own, "surf"))
    else:
        everything = lax.all_gather(own, "surf")
        tiles = jnp.concatenate(
            [own[None]]
            + [
                lax.dynamic_index_in_dim(
                    everything, (lax.axis_index("surf") + k) % tiles_count, 0
                )
                for k in range(1, tiles_count)
            ]
        )
    wide = width * tiles_count
    rest = wide - width
    acc_shape = (bodies, 8, width)
    points = VMEM(acc_shape, full)
    partial, velocity, own_features, codes = call(
        functools.partial(own_tile_kernel, bodies),
        [(HBM, pairs.T), (VMEM, own)],
        [
            (VMEM, acc_shape, full),
            (VMEM, (8, width), full),
            (VMEM, (bodies + 1, width, DEPTH), half),
            (VMEM, (code_rows(pair_count), 128), jnp.int32),
        ],
        scratch=(
            VMEM((bodies, 16, width), half),
            VMEM((width, 128), full),
            SMEM((2, pair_count), jnp.int32),
            SMEM((3,), jnp.int32),
            semaphore,
        ),
        units=3.0,
    )
    lower = lax.ppermute(tiles, "body", [(i, i + 1) for i in range(groups - 1)])
    upper = lax.ppermute(tiles, "body", [(i + 1, i) for i in range(groups - 1)])
    partial, features = call(
        functools.partial(group_kernel, bodies),
        [(VMEM, codes), (VMEM, tiles), (VMEM, partial), (VMEM, own_features)],
        [(VMEM, acc_shape, full), (VMEM, (bodies, wide, DEPTH), half)],
        scratch=(
            VMEM((bodies, 16, wide), half),
            VMEM((rest, 128), full),
            VMEM((rest, DEPTH), half),
            points,
        ),
        units=7.0,
    )
    potential, force = call(
        functools.partial(crossing_kernel, bodies),
        [(VMEM, codes), (VMEM, lower), (VMEM, upper), (VMEM, own), (VMEM, body_panels),
         (VMEM, body_normals), (VMEM, partial)],
        [(VMEM, acc_shape, full), (VMEM, (bodies, 8, 128), full)],
        scratch=(
            VMEM((2 * bodies, wide, DEPTH), half),
            VMEM((2 * bodies, 16, wide), half),
            points,
        ),
        units=6.0,
    )
    fs_next, own_potential = call(
        functools.partial(velocity_kernel, bodies),
        [(VMEM, tiles), (VMEM, features), (VMEM, velocity), (VMEM, fs_state), (VMEM, potential)],
        [(VMEM, (2, width), full), (HBM, acc_shape, full)],
        scratch=(VMEM((bodies, 16, rest), half), semaphore),
        units=5.0,
    )
    if tiles_count == 4:
        pieces = [force] + rotations(force, "surf")
    else:
        pieces = [lax.psum(force, "surf")] + [jnp.zeros_like(force)] * 3
    total, fs_next = call(
        finish_kernel,
        [(VMEM, piece) for piece in pieces] + [(VMEM, fs_next)],
        [(VMEM, (bodies, 3, 8), full), (VMEM, (2, width), full)],
    )
    return own_potential, total.transpose(0, 2, 1), fs_next


def solution(mesh):
    placed = (
        P(None, "body", "surf"),
        P(None, "body", "surf"),
        P(None, ("body", "surf")),
        P(None, ("body", "surf")),
        P(),
    )
    return jax.shard_map(
        on_device,
        mesh=mesh,
        in_specs=placed,
        out_specs=(P("body", None, "surf"), P("body", None, None), P(None, ("body", "surf"))),
        check_vma=False,
    )
```

```python
import functools

import jax
import jax.numpy as jnp
from jax import lax
from jax.experimental import pallas as pl
from jax.experimental.pallas import tpu as pltpu
from jax.sharding import PartitionSpec as P

soften = 0.01
gravity = 9.81
time_step = 0.2
mid_depth = -1.5
half = jnp.bfloat16
full = jnp.float32
DEPTH = 48


def rows_of(block_shape, rows):
    index = lax.broadcasted_iota(jnp.int32, block_shape, 0)
    block = jnp.zeros(block_shape, full)
    for position, row in enumerate(rows):
        block = jnp.where(index == position, row, block)
    return block


def three_parts(block):
    first = block.astype(half).astype(full)
    rest = block - first
    second = rest.astype(half).astype(full)
    return first, second, rest - second


def source_features(x, y, z):
    norm = x * x + y * y + z * z
    a, b, c = three_parts(rows_of((8, x.shape[1]), (x, y, z, norm, 1.0)))
    return jnp.concatenate([a, b, a, b, c, a], axis=0).T.astype(half)


def target_features(x, y, z):
    norm = x * x + y * y + z * z + soften
    a, b, c = three_parts(rows_of((8, x.shape[1]), (-2.0 * x, -2.0 * y, -2.0 * z, 1.0, norm)))
    return jnp.concatenate([a, a, b, b, a, c], axis=0).astype(half)


def two_parts(block):
    first = block.astype(half)
    return first, (block - first.astype(full)).astype(half)


def split_weights(block):
    first = block.astype(half).astype(full)
    return jnp.concatenate([first, block - first], axis=0).astype(half)


def product(left, right):
    return jnp.dot(left, right, preferred_element_type=full)


def weighted_sum(values, weights):
    high, low = two_parts(values)
    both = product(
        jnp.concatenate([weights, weights], axis=1), jnp.concatenate([high, low], axis=0)
    )
    return both[:8] + both[8:]


def influence_sum(targets, sources, weights):
    return weighted_sum(lax.rsqrt(product(sources, targets)), weights)


def point_row(bodies, member, axis):
    return 8 * bodies + 3 * member + axis


def surface_row(bodies, entry):
    return 11 * bodies + entry


def tile_rows(bodies):
    return -(-(11 * bodies + 3) // 8) * 8


def body_points(tile, bodies, member):
    return [
        tile[point_row(bodies, member, axis) : point_row(bodies, member, axis) + 1, :]
        for axis in range(3)
    ]


def surface_points(tile, bodies):
    x, y, weight = [
        tile[surface_row(bodies, entry) : surface_row(bodies, entry) + 1, :] for entry in range(3)
    ]
    return x, y, jnp.full_like(x, -mid_depth), weight


def shift_kernel(bodies, shift_ref):
    base = lax.axis_index("body") * bodies
    row = lax.broadcasted_iota(jnp.int32, shift_ref.shape, 0)
    shift_ref[...] = jnp.where(row < bodies, 2 * (base + row), 2 * base + bodies - 1).astype(full)


def pack_kernel(shift_ref, panels_ref, surface_ref, tile_ref):
    bodies, width = panels_ref.shape[1:]
    tile_ref[...] = jnp.zeros_like(tile_ref)
    area = panels_ref[3]
    for member in range(bodies):
        for entry in range(8):
            tile_ref[8 * member + entry : 8 * member + entry + 1, :] = (
                panels_ref[4 + entry, member : member + 1, :] * area[member : member + 1, :]
            )
        centre = shift_ref[member : member + 1, 0:1]
        for axis, shift in enumerate((centre, 0.0, mid_depth)):
            row = point_row(bodies, member, axis)
            tile_ref[row : row + 1, :] = panels_ref[axis, member : member + 1, :] - shift
    row = surface_row(bodies, 0)
    tile_ref[row : row + 1, :] = surface_ref[0:1, :] - shift_ref[bodies : bodies + 1, 0:1]
    tile_ref[row + 1 : row + 2, :] = surface_ref[1:2, :]
    tile_ref[row + 2 : row + 3, :] = surface_ref[2:3, :] * surface_ref[3:4, :]


def body_weights(tile, member):
    return split_weights(tile[8 * member : 8 * member + 8, :])


def moment_weights(tile, bodies, member):
    x, y, z = body_points(tile, bodies, member)
    first = tile[8 * member : 8 * member + 1, :]
    return split_weights(rows_of((8, x.shape[1]), (first, first * x, first * y, first * z)))


def prepare_tile(tile, bodies, columns, features, weights, spread):
    for member in range(bodies):
        features[member, columns, :] = source_features(*body_points(tile, bodies, member))
        weights[member, :, columns] = body_weights(tile, member)
    x, y, z, weight = surface_points(tile, bodies)
    features[bodies, columns, :] = source_features(x, y, z)
    spread[columns, :] = jnp.broadcast_to(weight, (128, x.shape[1])).T


def surface_sum(targets, sources, spread):
    values = lax.rsqrt(product(sources, targets))
    count, width = values.shape
    sums = []
    for start in range(0, width, 128):
        term = values[:, start : start + 128] * spread
        sums.append(jnp.sum(term.reshape(count // 8, 8, 128), axis=0))
    return jnp.sum(jnp.concatenate(sums, axis=1), axis=0, keepdims=True)


def velocity_term(features, weights, place, y, z):
    inverse = lax.rsqrt(product(features, target_features(place, y, z)))
    moments = weighted_sum(inverse * inverse * inverse, weights)
    return [
        moments[axis + 1 : axis + 2] - at * moments[0:1] for axis, at in enumerate((place, y, z))
    ]


def targets_of(points, member, shift):
    block = points[member]
    return target_features(block[0:1] + shift, block[1:2], block[2:3])


def code_rows(pair_count):
    return 4 * pair_count + 1


def own_tile_kernel(
    bodies, pairs_hbm, tile_ref, acc_ref, velocity_ref, features, codes,
    weights, spread, pairs, counts, sem,
):
    width = tile_ref.shape[1]
    copy = pltpu.make_async_copy(pairs_hbm, pairs, sem)
    copy.start()
    tile = tile_ref[...]
    prepare_tile(tile, bodies, pl.ds(0, width), features, weights, spread)
    x, y, z, _ = surface_points(tile, bodies)
    total = [jnp.zeros((1, width), full)] * 3
    index = lax.broadcasted_iota(jnp.int32, (8, width), 0)
    for member in range(bodies):
        point = body_points(tile, bodies, member)
        self_part = influence_sum(target_features(*point), features[member], weights[member])
        shift = float(2 * member - (bodies - 1))
        surface_part = surface_sum(
            target_features(point[0] + shift, point[1], point[2]), features[bodies], spread[...]
        )
        acc_ref[member] = self_part + jnp.where(index == 0, surface_part, 0.0)
        term = velocity_term(
            features[member], moment_weights(tile, bodies, member), x - shift, y, z
        )
        total = [so_far + part for so_far, part in zip(total, term)]
    velocity_ref[...] = rows_of((8, width), total)

    base = lax.axis_index("body") * bodies
    pair_count = pairs.shape[1]
    copy.wait()
    for entry in range(3):
        counts[entry] = 0

    def step_edge(step, carry):
        target = pairs[step % 2, step // 2] - base
        source = pairs[1 - step % 2, step // 2] - base

        @pl.when((target >= 0) & (target < bodies))
        def _():
            inside = (source >= 0) & (source < bodies)
            row = jnp.where(inside, 0, 1)
            slot = jnp.where(source < 0, source + bodies, source)
            place = counts[row]
            codes[pl.ds(row * 2 * pair_count + place, 1), :] = jnp.full(
                (1, 128), target * 16 + slot, jnp.int32
            )
            counts[row] = place + 1
            counts[2] = counts[2] | jnp.where(inside, 0, jnp.left_shift(1, slot))

        return carry

    lax.fori_loop(0, 2 * pair_count, step_edge, 0)
    lane = lax.broadcasted_iota(jnp.int32, (1, 128), 1)
    codes[4 * pair_count : 4 * pair_count + 1, :] = jnp.where(
        lane == 0, counts[0], jnp.where(lane == 1, counts[1], counts[2])
    )


def over_codes(codes, first, count, visit):
    def step_code(step, code):
        following = codes[first + step + 1, 0]
        visit(code // 16, code % 16)
        return following

    lax.fori_loop(0, count, step_code, codes[first, 0])


def group_kernel(
    bodies, codes, tiles_ref, given_ref, own_features, acc_ref, features, weights, spread, surface, points
):
    count, _, width = tiles_ref.shape
    rest = (count - 1) * width
    pair_count = codes.shape[0] // 4
    for index in range(1, count):
        tile = tiles_ref[index]
        columns = pl.ds((index - 1) * width, width)
        for member in range(bodies):
            features[member, columns, :] = source_features(*body_points(tile, bodies, member))
            weights[member, :, columns] = body_weights(tile, member)
        x, y, z, weight = surface_points(tile, bodies)
        surface[columns, :] = source_features(x, y, z)
        spread[columns, :] = jnp.broadcast_to(weight, (128, width)).T
    own = tiles_ref[0]
    for member in range(bodies):
        points[member] = rows_of((8, width), body_points(own, bodies, member))
        features[member, rest:, :] = own_features[member]
        weights[member, :, rest:] = body_weights(own, member)

    def own_step(member, carry):
        acc_ref[member] = given_ref[member] + influence_sum(
            targets_of(points, member, 0.0), features[member, :rest, :], weights[member, :, :rest]
        )
        shift = (2 * member - (bodies - 1)).astype(full)
        acc_ref[member, 0:1, :] += surface_sum(
            targets_of(points, member, shift), surface[...], spread[...]
        )
        return carry

    lax.fori_loop(0, bodies, own_step, 0)

    def visit(target, source):
        shift = (2 * (target - source)).astype(full)
        acc_ref[target] += influence_sum(
            targets_of(points, target, shift), features[source], weights[source]
        )

    over_codes(codes, 0, codes[4 * pair_count, 0], visit)


def crossing_kernel(
    bodies, codes, lower_ref, upper_ref, tile_ref, panels_ref, normals_ref, given_ref,
    acc_ref, force_ref, features, weights, points,
):
    count, _, width = lower_ref.shape
    pair_count = codes.shape[0] // 4
    used = codes[4 * pair_count, 2]
    crossings = codes[4 * pair_count, 1]
    own = tile_ref[...]
    for member in range(bodies):
        points[member] = rows_of((8, width), body_points(own, bodies, member))
    acc_ref[...] = given_ref[...]
    force_ref[...] = jnp.zeros_like(force_ref)
    for slot in range(2 * bodies):

        @pl.when((jnp.right_shift(used, slot) & 1) == 1)
        def _():
            side = lower_ref if slot < bodies else upper_ref
            for index in range(count):
                columns = pl.ds(index * width, width)
                tile = side[index]
                member = slot % bodies
                features[slot, columns, :] = source_features(*body_points(tile, bodies, member))
                weights[slot, :, columns] = body_weights(tile, member)

    def visit(target, slot):
        source = jnp.where(slot < bodies, slot - bodies, slot)
        shift = (2 * (target - source)).astype(full)
        acc_ref[target] += influence_sum(
            targets_of(points, target, shift), features[slot], weights[slot]
        )

    over_codes(codes, 2 * pair_count, crossings, visit)
    for member in range(bodies):
        area = panels_ref[3, member : member + 1, :]
        scaled = rows_of(
            (8, width), [normals_ref[axis, member : member + 1, :] * area for axis in range(3)]
        )
        force_ref[member, :, 0:8] = lax.dot_general(
            scaled,
            acc_ref[member],
            (((1,), (1,)), ((), ())),
            precision=lax.Precision.HIGHEST,
            preferred_element_type=full,
        )


def velocity_kernel(
    bodies, tiles_ref, features, given_ref, state_ref, potential_ref, next_ref, potential_hbm, weights, sem
):
    count, _, width = tiles_ref.shape
    rest = (count - 1) * width
    store = pltpu.make_async_copy(potential_ref, potential_hbm, sem)
    store.start()
    for index in range(1, count):
        tile = tiles_ref[index]
        for member in range(bodies):
            weights[member, :, pl.ds((index - 1) * width, width)] = moment_weights(
                tile, bodies, member
            )
    own = tiles_ref[0]
    x, y, z, _ = surface_points(own, bodies)

    def body_step(member, velocity):
        place = x + (bodies - 1 - 2 * member).astype(full)
        term = velocity_term(features[member, :rest, :], weights[member], place, y, z)
        return tuple(so_far + part for so_far, part in zip(velocity, term))

    start = tuple(given_ref[axis : axis + 1, :] for axis in range(3))
    velocity = lax.fori_loop(0, bodies, body_step, start)
    speed_sq = velocity[0] * velocity[0] + velocity[1] * velocity[1] + velocity[2] * velocity[2]
    potential, elevation = state_ref[0:1, :], state_ref[1:2, :]
    next_ref[0:1, :] = potential + time_step * (-gravity * elevation - 0.5 * speed_sq)
    next_ref[1:2, :] = elevation + time_step * velocity[2]
    store.wait()


def finish_kernel(own_ref, first_ref, second_ref, third_ref, next_ref, force_ref, out_ref):
    total = (own_ref[...] + second_ref[...]) + (first_ref[...] + third_ref[...])
    force_ref[...] = total[:, :3, :8]
    out_ref[...] = next_ref[...]


VMEM, SMEM, HBM = pltpu.VMEM, pltpu.SMEM, pltpu.HBM


def call(kernel, operands, results, scratch=(), units=0.0):
    single = len(results) == 1
    out = pl.pallas_call(
        kernel,
        out_shape=[jax.ShapeDtypeStruct(shape, kind) for _, shape, kind in results],
        in_specs=[pl.BlockSpec(memory_space=space) for space, _ in operands],
        out_specs=[pl.BlockSpec(memory_space=space) for space, _, _ in results],
        scratch_shapes=list(scratch),
        compiler_params=pltpu.CompilerParams(vmem_limit_bytes=40 * 1024 * 1024),
        cost_estimate=pl.CostEstimate(
            flops=int(units * 1.2e9), bytes_accessed=1024, transcendentals=0
        ),
    )(*[array for _, array in operands])
    return out[0] if single else out


def rotations(block, axis):
    count = lax.axis_size(axis)
    return [
        lax.ppermute(block, axis, [(i, (i + k) % count) for i in range(count)])
        for k in range(1, count)
    ]


def on_device(body_panels, body_normals, fs_panels, fs_state, pairs):
    bodies = body_panels.shape[1]
    width = body_panels.shape[2]
    tiles_count = lax.axis_size("surf")
    groups = lax.axis_size("body")
    pair_count = pairs.shape[0]
    semaphore = pltpu.SemaphoreType.DMA
    shifts = call(
        functools.partial(shift_kernel, bodies), [], [(VMEM, (8, 128), full)], units=2.0
    )
    own = call(
        pack_kernel,
        [(VMEM, shifts), (VMEM, body_panels), (VMEM, fs_panels)],
        [(VMEM, (tile_rows(bodies), width), full)],
    )
    if tiles_count == 4:
        tiles = jnp.stack([own] + rotations(own, "surf"))
    else:
        everything = lax.all_gather(own, "surf")
        tiles = jnp.concatenate(
            [own[None]]
            + [
                lax.dynamic_index_in_dim(
                    everything, (lax.axis_index("surf") + k) % tiles_count, 0
                )
                for k in range(1, tiles_count)
            ]
        )
    wide = width * tiles_count
    rest = wide - width
    acc_shape = (bodies, 8, width)
    points = VMEM(acc_shape, full)
    partial, velocity, own_features, codes = call(
        functools.partial(own_tile_kernel, bodies),
        [(HBM, pairs.T), (VMEM, own)],
        [
            (VMEM, acc_shape, full),
            (VMEM, (8, width), full),
            (VMEM, (bodies + 1, width, DEPTH), half),
            (VMEM, (code_rows(pair_count), 128), jnp.int32),
        ],
        scratch=(
            VMEM((bodies, 16, width), half),
            VMEM((width, 128), full),
            SMEM((2, pair_count), jnp.int32),
            SMEM((3,), jnp.int32),
            semaphore,
        ),
        units=3.0,
    )
    lower = lax.ppermute(tiles, "body", [(i, i + 1) for i in range(groups - 1)])
    upper = lax.ppermute(tiles, "body", [(i + 1, i) for i in range(groups - 1)])
    partial, features = call(
        functools.partial(group_kernel, bodies),
        [(VMEM, codes), (VMEM, tiles), (VMEM, partial), (VMEM, own_features)],
        [(VMEM, acc_shape, full), (VMEM, (bodies, wide, DEPTH), half)],
        scratch=(
            VMEM((bodies, 16, wide), half),
            VMEM((rest, 128), full),
            VMEM((rest, DEPTH), half),
            points,
        ),
        units=7.0,
    )
    potential, force = call(
        functools.partial(crossing_kernel, bodies),
        [(VMEM, codes), (VMEM, lower), (VMEM, upper), (VMEM, own), (VMEM, body_panels),
         (VMEM, body_normals), (VMEM, partial)],
        [(VMEM, acc_shape, full), (VMEM, (bodies, 8, 128), full)],
        scratch=(
            VMEM((2 * bodies, wide, DEPTH), half),
            VMEM((2 * bodies, 16, wide), half),
            points,
        ),
        units=6.0,
    )
    fs_next, own_potential = call(
        functools.partial(velocity_kernel, bodies),
        [(VMEM, tiles), (VMEM, features), (VMEM, velocity), (VMEM, fs_state), (VMEM, potential)],
        [(VMEM, (2, width), full), (HBM, acc_shape, full)],
        scratch=(VMEM((bodies, 16, rest), half), semaphore),
        units=5.0,
    )
    if tiles_count == 4:
        pieces = [force] + rotations(force, "surf")
    else:
        pieces = [lax.psum(force, "surf")] + [jnp.zeros_like(force)] * 3
    total, fs_next = call(
        finish_kernel,
        [(VMEM, piece) for piece in pieces] + [(VMEM, fs_next)],
        [(VMEM, (bodies, 3, 8), full), (VMEM, (2, width), full)],
    )
    return own_potential, total.transpose(0, 2, 1), fs_next


def solution(mesh):
    placed = (
        P(None, "body", "surf"),
        P(None, "body", "surf"),
        P(None, ("body", "surf")),
        P(None, ("body", "surf")),
        P(),
    )
    return jax.shard_map(
        on_device,
        mesh=mesh,
        in_specs=placed,
        out_specs=(P("body", None, "surf"), P("body", None, None), P(None, ("body", "surf"))),
        check_vma=False,
    )
```

```python
import functools

import jax
import jax.numpy as jnp
from jax import lax
from jax.experimental import pallas as pl
from jax.experimental.pallas import tpu as pltpu
from jax.sharding import PartitionSpec as P

soften = 0.01
gravity = 9.81
time_step = 0.2
mid_depth = -1.5
half = jnp.bfloat16
full = jnp.float32
DEPTH = 48


def rows_of(block_shape, rows):
    index = lax.broadcasted_iota(jnp.int32, block_shape, 0)
    block = jnp.zeros(block_shape, full)
    for position, row in enumerate(rows):
        block = jnp.where(index == position, row, block)
    return block


def three_parts(block):
    first = block.astype(half).astype(full)
    rest = block - first
    second = rest.astype(half).astype(full)
    return first, second, rest - second


def source_features(x, y, z):
    norm = x * x + y * y + z * z
    a, b, c = three_parts(rows_of((8, x.shape[1]), (x, y, z, norm, 1.0)))
    return jnp.concatenate([a, b, a, b, c, a], axis=0).T.astype(half)


def target_features(x, y, z):
    norm = x * x + y * y + z * z + soften
    a, b, c = three_parts(rows_of((8, x.shape[1]), (-2.0 * x, -2.0 * y, -2.0 * z, 1.0, norm)))
    return jnp.concatenate([a, a, b, b, a, c], axis=0).astype(half)


def two_parts(block):
    first = block.astype(half)
    return first, (block - first.astype(full)).astype(half)


def split_weights(block):
    first = block.astype(half).astype(full)
    return jnp.concatenate([first, block - first], axis=0).astype(half)


def product(left, right):
    return jnp.dot(left, right, preferred_element_type=full)


def weighted_sum(values, weights):
    high, low = two_parts(values)
    both = product(
        jnp.concatenate([weights, weights], axis=1), jnp.concatenate([high, low], axis=0)
    )
    return both[:8] + both[8:]


def influence_sum(targets, sources, weights):
    return weighted_sum(lax.rsqrt(product(sources, targets)), weights)


def point_row(bodies, member, axis):
    return 8 * bodies + 3 * member + axis


def surface_row(bodies, entry):
    return 11 * bodies + entry


def tile_rows(bodies):
    return -(-(11 * bodies + 3) // 8) * 8


def body_points(tile, bodies, member):
    return [
        tile[point_row(bodies, member, axis) : point_row(bodies, member, axis) + 1, :]
        for axis in range(3)
    ]


def surface_points(tile, bodies):
    x, y, weight = [
        tile[surface_row(bodies, entry) : surface_row(bodies, entry) + 1, :] for entry in range(3)
    ]
    return x, y, jnp.full_like(x, -mid_depth), weight


def shift_kernel(bodies, shift_ref):
    base = lax.axis_index("body") * bodies
    row = lax.broadcasted_iota(jnp.int32, shift_ref.shape, 0)
    shift_ref[...] = jnp.where(row < bodies, 2 * (base + row), 2 * base + bodies - 1).astype(full)


def pack_kernel(shift_ref, panels_ref, surface_ref, tile_ref):
    bodies, width = panels_ref.shape[1:]
    tile_ref[...] = jnp.zeros_like(tile_ref)
    area = panels_ref[3]
    for member in range(bodies):
        for entry in range(8):
            tile_ref[8 * member + entry : 8 * member + entry + 1, :] = (
                panels_ref[4 + entry, member : member + 1, :] * area[member : member + 1, :]
            )
        centre = shift_ref[member : member + 1, 0:1]
        for axis, shift in enumerate((centre, 0.0, mid_depth)):
            row = point_row(bodies, member, axis)
            tile_ref[row : row + 1, :] = panels_ref[axis, member : member + 1, :] - shift
    row = surface_row(bodies, 0)
    tile_ref[row : row + 1, :] = surface_ref[0:1, :] - shift_ref[bodies : bodies + 1, 0:1]
    tile_ref[row + 1 : row + 2, :] = surface_ref[1:2, :]
    tile_ref[row + 2 : row + 3, :] = surface_ref[2:3, :] * surface_ref[3:4, :]


def body_weights(tile, member):
    return split_weights(tile[8 * member : 8 * member + 8, :])


def moment_weights(tile, bodies, member):
    x, y, z = body_points(tile, bodies, member)
    first = tile[8 * member : 8 * member + 1, :]
    return split_weights(rows_of((8, x.shape[1]), (first, first * x, first * y, first * z)))


def prepare_tile(tile, bodies, columns, features, weights, spread):
    for member in range(bodies):
        features[member, columns, :] = source_features(*body_points(tile, bodies, member))
        weights[member, :, columns] = body_weights(tile, member)
    x, y, z, weight = surface_points(tile, bodies)
    features[bodies, columns, :] = source_features(x, y, z)
    spread[columns, :] = jnp.broadcast_to(weight, (128, x.shape[1])).T


def surface_sum(targets, sources, spread):
    values = lax.rsqrt(product(sources, targets))
    count, width = values.shape
    sums = []
    for start in range(0, width, 128):
        term = values[:, start : start + 128] * spread
        sums.append(jnp.sum(term.reshape(count // 8, 8, 128), axis=0))
    return jnp.sum(jnp.concatenate(sums, axis=1), axis=0, keepdims=True)


def velocity_term(features, weights, place, y, z):
    inverse = lax.rsqrt(product(features, target_features(place, y, z)))
    moments = weighted_sum(inverse * inverse * inverse, weights)
    return [
        moments[axis + 1 : axis + 2] - at * moments[0:1] for axis, at in enumerate((place, y, z))
    ]


def targets_of(points, member, shift):
    block = points[member]
    return target_features(block[0:1] + shift, block[1:2], block[2:3])


def code_rows(pair_count):
    return 4 * pair_count + 1


def own_tile_kernel(
    bodies, pairs_hbm, tile_ref, acc_ref, velocity_ref, features, codes,
    weights, spread, pairs, counts, sem,
):
    width = tile_ref.shape[1]
    copy = pltpu.make_async_copy(pairs_hbm, pairs, sem)
    copy.start()
    tile = tile_ref[...]
    prepare_tile(tile, bodies, pl.ds(0, width), features, weights, spread)
    x, y, z, _ = surface_points(tile, bodies)
    total = [jnp.zeros((1, width), full)] * 3
    index = lax.broadcasted_iota(jnp.int32, (8, width), 0)
    for member in range(bodies):
        point = body_points(tile, bodies, member)
        self_part = influence_sum(target_features(*point), features[member], weights[member])
        shift = float(2 * member - (bodies - 1))
        surface_part = surface_sum(
            target_features(point[0] + shift, point[1], point[2]), features[bodies], spread[...]
        )
        acc_ref[member] = self_part + jnp.where(index == 0, surface_part, 0.0)
        term = velocity_term(
            features[member], moment_weights(tile, bodies, member), x - shift, y, z
        )
        total = [so_far + part for so_far, part in zip(total, term)]
    velocity_ref[...] = rows_of((8, width), total)

    base = lax.axis_index("body") * bodies
    pair_count = pairs.shape[1]
    copy.wait()
    for entry in range(3):
        counts[entry] = 0

    def step_edge(step, carry):
        target = pairs[step % 2, step // 2] - base
        source = pairs[1 - step % 2, step // 2] - base

        @pl.when((target >= 0) & (target < bodies))
        def _():
            inside = (source >= 0) & (source < bodies)
            row = jnp.where(inside, 0, 1)
            slot = jnp.where(inside, source, neighbour_slot(bodies, source))
            place = counts[row]
            codes[pl.ds(row * 2 * pair_count + place, 1), :] = jnp.full(
                (1, 128), target * 16 + slot, jnp.int32
            )
            counts[row] = place + 1
            counts[2] = counts[2] | jnp.where(inside, 0, jnp.left_shift(1, slot))

        return carry

    lax.fori_loop(0, 2 * pair_count, step_edge, 0)
    lane = lax.broadcasted_iota(jnp.int32, (1, 128), 1)
    codes[4 * pair_count : 4 * pair_count + 1, :] = jnp.where(
        lane == 0, counts[0], jnp.where(lane == 1, counts[1], counts[2])
    )


def neighbour_slot(bodies, source):
    upper = (source >= bodies).astype(jnp.int32)
    second = (upper + lax.axis_index("body")) % 2 == 0
    return jnp.where(upper == 1, source - bodies, source + bodies) + jnp.where(second, bodies, 0)


def slot_source(bodies, slot):
    second = (slot >= bodies).astype(jnp.int32)
    upper = (second + lax.axis_index("body")) % 2 == 0
    return slot - second * bodies + jnp.where(upper, bodies, -bodies)


def over_codes(codes, first, count, visit):
    def step_code(step, code):
        following = codes[first + step + 1, 0]
        visit(code // 16, code % 16)
        return following

    lax.fori_loop(0, count, step_code, codes[first, 0])


def group_kernel(
    bodies, codes, tiles_ref, given_ref, own_features, acc_ref, features, weights, spread, surface, points
):
    count, _, width = tiles_ref.shape
    rest = (count - 1) * width
    pair_count = codes.shape[0] // 4
    for index in range(1, count):
        tile = tiles_ref[index]
        columns = pl.ds((index - 1) * width, width)
        for member in range(bodies):
            features[member, columns, :] = source_features(*body_points(tile, bodies, member))
            weights[member, :, columns] = body_weights(tile, member)
        x, y, z, weight = surface_points(tile, bodies)
        surface[columns, :] = source_features(x, y, z)
        spread[columns, :] = jnp.broadcast_to(weight, (128, width)).T
    own = tiles_ref[0]
    for member in range(bodies):
        points[member] = rows_of((8, width), body_points(own, bodies, member))
        features[member, rest:, :] = own_features[member]
        weights[member, :, rest:] = body_weights(own, member)

    def own_step(member, carry):
        acc_ref[member] = given_ref[member] + influence_sum(
            targets_of(points, member, 0.0), features[member, :rest, :], weights[member, :, :rest]
        )
        shift = (2 * member - (bodies - 1)).astype(full)
        acc_ref[member, 0:1, :] += surface_sum(
            targets_of(points, member, shift), surface[...], spread[...]
        )
        return carry

    lax.fori_loop(0, bodies, own_step, 0)

    def visit(target, source):
        shift = (2 * (target - source)).astype(full)
        acc_ref[target] += influence_sum(
            targets_of(points, target, shift), features[source], weights[source]
        )

    over_codes(codes, 0, codes[4 * pair_count, 0], visit)


def crossing_kernel(
    bodies, codes, first_ref, second_ref, tile_ref, panels_ref, normals_ref, given_ref,
    acc_ref, force_ref, features, weights, points,
):
    count, _, width = first_ref.shape
    pair_count = codes.shape[0] // 4
    used = codes[4 * pair_count, 2]
    crossings = codes[4 * pair_count, 1]
    own = tile_ref[...]
    for member in range(bodies):
        points[member] = rows_of((8, width), body_points(own, bodies, member))
    acc_ref[...] = given_ref[...]
    force_ref[...] = jnp.zeros_like(force_ref)
    for slot in range(2 * bodies):

        @pl.when((jnp.right_shift(used, slot) & 1) == 1)
        def _():
            side = first_ref if slot < bodies else second_ref
            for index in range(count):
                columns = pl.ds(index * width, width)
                tile = side[index]
                member = slot % bodies
                features[slot, columns, :] = source_features(*body_points(tile, bodies, member))
                weights[slot, :, columns] = body_weights(tile, member)

    def visit(target, slot):
        source = slot_source(bodies, slot)
        shift = (2 * (target - source)).astype(full)
        acc_ref[target] += influence_sum(
            targets_of(points, target, shift), features[slot], weights[slot]
        )

    over_codes(codes, 2 * pair_count, crossings, visit)
    for member in range(bodies):
        area = panels_ref[3, member : member + 1, :]
        scaled = rows_of(
            (8, width), [normals_ref[axis, member : member + 1, :] * area for axis in range(3)]
        )
        force_ref[member, :, 0:8] = lax.dot_general(
            scaled,
            acc_ref[member],
            (((1,), (1,)), ((), ())),
            precision=lax.Precision.HIGHEST,
            preferred_element_type=full,
        )


def velocity_kernel(
    bodies, tiles_ref, features, given_ref, state_ref, potential_ref, next_ref, potential_hbm, weights, sem
):
    count, _, width = tiles_ref.shape
    rest = (count - 1) * width
    store = pltpu.make_async_copy(potential_ref, potential_hbm, sem)
    store.start()
    for index in range(1, count):
        tile = tiles_ref[index]
        for member in range(bodies):
            weights[member, :, pl.ds((index - 1) * width, width)] = moment_weights(
                tile, bodies, member
            )
    own = tiles_ref[0]
    x, y, z, _ = surface_points(own, bodies)

    def body_step(member, velocity):
        place = x + (bodies - 1 - 2 * member).astype(full)
        term = velocity_term(features[member, :rest, :], weights[member], place, y, z)
        return tuple(so_far + part for so_far, part in zip(velocity, term))

    start = tuple(given_ref[axis : axis + 1, :] for axis in range(3))
    velocity = lax.fori_loop(0, bodies, body_step, start)
    speed_sq = velocity[0] * velocity[0] + velocity[1] * velocity[1] + velocity[2] * velocity[2]
    potential, elevation = state_ref[0:1, :], state_ref[1:2, :]
    next_ref[0:1, :] = potential + time_step * (-gravity * elevation - 0.5 * speed_sq)
    next_ref[1:2, :] = elevation + time_step * velocity[2]
    store.wait()


def finish_kernel(own_ref, first_ref, second_ref, third_ref, next_ref, force_ref, out_ref):
    total = (own_ref[...] + second_ref[...]) + (first_ref[...] + third_ref[...])
    force_ref[...] = total[:, :3, :8]
    out_ref[...] = next_ref[...]


VMEM, SMEM, HBM = pltpu.VMEM, pltpu.SMEM, pltpu.HBM


def call(kernel, operands, results, scratch=(), units=0.0):
    single = len(results) == 1
    out = pl.pallas_call(
        kernel,
        out_shape=[jax.ShapeDtypeStruct(shape, kind) for _, shape, kind in results],
        in_specs=[pl.BlockSpec(memory_space=space) for space, _ in operands],
        out_specs=[pl.BlockSpec(memory_space=space) for space, _, _ in results],
        scratch_shapes=list(scratch),
        compiler_params=pltpu.CompilerParams(vmem_limit_bytes=40 * 1024 * 1024),
        cost_estimate=pl.CostEstimate(
            flops=int(units * 1.2e9), bytes_accessed=1024, transcendentals=0
        ),
    )(*[array for _, array in operands])
    return out[0] if single else out


def rotations(block, axis):
    count = lax.axis_size(axis)
    return [
        lax.ppermute(block, axis, [(i, (i + k) % count) for i in range(count)])
        for k in range(1, count)
    ]


def exchanges(block, axis):
    count = lax.axis_size(axis)
    return [lax.ppermute(block, axis, [(i, i ^ k) for i in range(count)]) for k in range(1, count)]


def on_device(body_panels, body_normals, fs_panels, fs_state, pairs):
    bodies = body_panels.shape[1]
    width = body_panels.shape[2]
    tiles_count = lax.axis_size("surf")
    groups = lax.axis_size("body")
    pair_count = pairs.shape[0]
    semaphore = pltpu.SemaphoreType.DMA
    shifts = call(
        functools.partial(shift_kernel, bodies), [], [(VMEM, (8, 128), full)], units=2.0
    )
    own = call(
        pack_kernel,
        [(VMEM, shifts), (VMEM, body_panels), (VMEM, fs_panels)],
        [(VMEM, (tile_rows(bodies), width), full)],
    )
    if tiles_count == 4:
        tiles = jnp.stack([own] + exchanges(own, "surf"))
    else:
        everything = lax.all_gather(own, "surf")
        tiles = jnp.concatenate(
            [own[None]]
            + [
                lax.dynamic_index_in_dim(
                    everything, (lax.axis_index("surf") + k) % tiles_count, 0
                )
                for k in range(1, tiles_count)
            ]
        )
    wide = width * tiles_count
    rest = wide - width
    acc_shape = (bodies, 8, width)
    points = VMEM(acc_shape, full)
    partial, velocity, own_features, codes = call(
        functools.partial(own_tile_kernel, bodies),
        [(HBM, pairs.T), (VMEM, own)],
        [
            (VMEM, acc_shape, full),
            (VMEM, (8, width), full),
            (VMEM, (bodies + 1, width, DEPTH), half),
            (VMEM, (code_rows(pair_count), 128), jnp.int32),
        ],
        scratch=(
            VMEM((bodies, 16, width), half),
            VMEM((width, 128), full),
            SMEM((2, pair_count), jnp.int32),
            SMEM((3,), jnp.int32),
            semaphore,
        ),
        units=3.0,
    )
    first, second = [
        lax.ppermute(
            tiles,
            "body",
            [pair for i in range(start, groups - 1, 2) for pair in ((i, i + 1), (i + 1, i))],
        )
        for start in (0, 1)
    ]
    partial, features = call(
        functools.partial(group_kernel, bodies),
        [(VMEM, codes), (VMEM, tiles), (VMEM, partial), (VMEM, own_features)],
        [(VMEM, acc_shape, full), (VMEM, (bodies, wide, DEPTH), half)],
        scratch=(
            VMEM((bodies, 16, wide), half),
            VMEM((rest, 128), full),
            VMEM((rest, DEPTH), half),
            points,
        ),
        units=7.0,
    )
    potential, force = call(
        functools.partial(crossing_kernel, bodies),
        [(VMEM, codes), (VMEM, first), (VMEM, second), (VMEM, own), (VMEM, body_panels),
         (VMEM, body_normals), (VMEM, partial)],
        [(VMEM, acc_shape, full), (VMEM, (bodies, 8, 128), full)],
        scratch=(
            VMEM((2 * bodies, wide, DEPTH), half),
            VMEM((2 * bodies, 16, wide), half),
            points,
        ),
        units=6.0,
    )
    fs_next, own_potential = call(
        functools.partial(velocity_kernel, bodies),
        [(VMEM, tiles), (VMEM, features), (VMEM, velocity), (VMEM, fs_state), (VMEM, potential)],
        [(VMEM, (2, width), full), (HBM, acc_shape, full)],
        scratch=(VMEM((bodies, 16, rest), half), semaphore),
        units=5.0,
    )
    if tiles_count == 4:
        pieces = [force] + rotations(force, "surf")
    else:
        pieces = [lax.psum(force, "surf")] + [jnp.zeros_like(force)] * 3
    total, fs_next = call(
        finish_kernel,
        [(VMEM, piece) for piece in pieces] + [(VMEM, fs_next)],
        [(VMEM, (bodies, 3, 8), full), (VMEM, (2, width), full)],
    )
    return own_potential, total.transpose(0, 2, 1), fs_next


def solution(mesh):
    placed = (
        P(None, "body", "surf"),
        P(None, "body", "surf"),
        P(None, ("body", "surf")),
        P(None, ("body", "surf")),
        P(),
    )
    return jax.shard_map(
        on_device,
        mesh=mesh,
        in_specs=placed,
        out_specs=(P("body", None, "surf"), P("body", None, None), P(None, ("body", "surf"))),
        check_vma=False,
    )
```

```python
import functools

import jax
import jax.numpy as jnp
from jax import lax
from jax.experimental import pallas as pl
from jax.experimental.pallas import tpu as pltpu
from jax.sharding import PartitionSpec as P

soften = 0.01
gravity = 9.81
time_step = 0.2
mid_depth = -1.5
half = jnp.bfloat16
full = jnp.float32
DEPTH = 48


def rows_of(block_shape, rows):
    index = lax.broadcasted_iota(jnp.int32, block_shape, 0)
    block = jnp.zeros(block_shape, full)
    for position, row in enumerate(rows):
        block = jnp.where(index == position, row, block)
    return block


def three_parts(block):
    first = block.astype(half).astype(full)
    rest = block - first
    second = rest.astype(half).astype(full)
    return first, second, rest - second


def source_features(x, y, z):
    norm = x * x + y * y + z * z
    a, b, c = three_parts(rows_of((8, x.shape[1]), (x, y, z, norm, 1.0)))
    return jnp.concatenate([a, b, a, b, c, a], axis=0).astype(half).T


def target_features(x, y, z):
    norm = x * x + y * y + z * z + soften
    a, b, c = three_parts(rows_of((8, x.shape[1]), (-2.0 * x, -2.0 * y, -2.0 * z, 1.0, norm)))
    return jnp.concatenate([a, a, b, b, a, c], axis=0).astype(half)


def two_parts(block):
    first = block.astype(half)
    return first, (block - first.astype(full)).astype(half)


def split_weights(block):
    first = block.astype(half).astype(full)
    return jnp.concatenate([first, block - first], axis=0).astype(half)


def product(left, right):
    return jnp.dot(left, right, preferred_element_type=full)


def weighted_sum(values, weights):
    high, low = two_parts(values)
    both = product(
        jnp.concatenate([weights, weights], axis=1), jnp.concatenate([high, low], axis=0)
    )
    return both[:8] + both[8:]


def influence_sum(targets, sources, weights):
    return weighted_sum(lax.rsqrt(product(sources, targets)), weights)


LANES = 128


def tile_rows(bodies, width):
    return -(-(11 * bodies + 3) * (width // LANES) // 8) * 8


def weight_rows(blocks, member, block):
    start = 8 * (member * blocks + block)
    return slice(start, start + 8)


def entry_row(bodies, blocks, block, entry):
    row = 8 * bodies * blocks + (3 * bodies + 3) * block + entry
    return slice(row, row + 1)


def tile_entry(tile, bodies, blocks, entry):
    return jnp.concatenate(
        [tile[entry_row(bodies, blocks, block, entry), :] for block in range(blocks)], axis=1
    )


def tile_weights(tile, blocks, member):
    return jnp.concatenate(
        [tile[weight_rows(blocks, member, block), :] for block in range(blocks)], axis=1
    )


def body_points(tile, bodies, blocks, member):
    return [tile_entry(tile, bodies, blocks, 3 * member + axis) for axis in range(3)]


def surface_points(tile, bodies, blocks):
    x, y, weight = [tile_entry(tile, bodies, blocks, 3 * bodies + entry) for entry in range(3)]
    return x, y, jnp.full_like(x, -mid_depth), weight


def shift_kernel(bodies, shift_ref):
    base = lax.axis_index("body") * bodies
    row = lax.broadcasted_iota(jnp.int32, shift_ref.shape, 0)
    shift_ref[...] = jnp.where(row < bodies, 2 * (base + row), 2 * base + bodies - 1).astype(full)


def pack_kernel(shift_ref, panels_ref, surface_ref, tile_ref):
    bodies, width = panels_ref.shape[1:]
    blocks = width // LANES
    if tile_ref.shape[0] > (11 * bodies + 3) * blocks:
        tile_ref[...] = jnp.zeros_like(tile_ref)
    for block in range(blocks):
        lanes = slice(block * LANES, (block + 1) * LANES)
        for member in range(bodies):
            row = slice(member, member + 1)
            area = panels_ref[3, row, lanes]
            rows = weight_rows(blocks, member, block)
            for entry in range(8):
                place = rows.start + entry
                tile_ref[place : place + 1, :] = panels_ref[4 + entry, row, lanes] * area
            for axis, shift in enumerate((shift_ref[row, 0:1], 0.0, mid_depth)):
                tile_ref[entry_row(bodies, blocks, block, 3 * member + axis), :] = (
                    panels_ref[axis, row, lanes] - shift
                )
        surface = (
            surface_ref[0:1, lanes] - shift_ref[bodies : bodies + 1, 0:1],
            surface_ref[1:2, lanes],
            surface_ref[2:3, lanes] * surface_ref[3:4, lanes],
        )
        for entry, value in enumerate(surface):
            tile_ref[entry_row(bodies, blocks, block, 3 * bodies + entry), :] = value


def body_weights(tile, blocks, member):
    return split_weights(tile_weights(tile, blocks, member))


def moment_weights(tile, bodies, blocks, member):
    x, y, z = body_points(tile, bodies, blocks, member)
    first = tile_weights(tile, blocks, member)[0:1, :]
    return split_weights(rows_of((8, x.shape[1]), (first, first * x, first * y, first * z)))


def prepare_tile(tile, bodies, blocks, columns, features, weights, spread):
    for member in range(bodies):
        features[member, columns, :] = source_features(*body_points(tile, bodies, blocks, member))
        weights[member, :, columns] = body_weights(tile, blocks, member)
    x, y, z, weight = surface_points(tile, bodies, blocks)
    features[bodies, columns, :] = source_features(x, y, z)
    spread[columns, :] = jnp.broadcast_to(weight, (128, x.shape[1])).T


def surface_sum(targets, sources, spread):
    values = lax.rsqrt(product(sources, targets))
    count, width = values.shape
    sums = []
    for start in range(0, width, 128):
        term = values[:, start : start + 128] * spread
        sums.append(jnp.sum(term.reshape(count // 8, 8, 128), axis=0))
    return jnp.sum(jnp.concatenate(sums, axis=1), axis=0, keepdims=True)


def velocity_term(features, weights, place, y, z):
    inverse = lax.rsqrt(product(features, target_features(place, y, z)))
    moments = weighted_sum(inverse * inverse * inverse, weights)
    return [
        moments[axis + 1 : axis + 2] - at * moments[0:1] for axis, at in enumerate((place, y, z))
    ]


def targets_of(points, member, shift):
    block = points[member]
    return target_features(block[0:1] + shift, block[1:2], block[2:3])


def code_rows(pair_count):
    return 4 * pair_count + 1


def own_tile_kernel(
    bodies, pairs_hbm, tile_ref, acc_ref, velocity_ref, features, codes,
    weights, spread, pairs, counts, sem,
):
    width = acc_ref.shape[2]
    blocks = width // LANES
    copy = pltpu.make_async_copy(pairs_hbm, pairs, sem)
    copy.start()
    tile = tile_ref[...]
    prepare_tile(tile, bodies, blocks, pl.ds(0, width), features, weights, spread)
    x, y, z, _ = surface_points(tile, bodies, blocks)
    total = [jnp.zeros((1, width), full)] * 3
    index = lax.broadcasted_iota(jnp.int32, (8, width), 0)
    for member in range(bodies):
        point = body_points(tile, bodies, blocks, member)
        self_part = influence_sum(target_features(*point), features[member], weights[member])
        shift = float(2 * member - (bodies - 1))
        surface_part = surface_sum(
            target_features(point[0] + shift, point[1], point[2]), features[bodies], spread[...]
        )
        acc_ref[member] = self_part + jnp.where(index == 0, surface_part, 0.0)
        term = velocity_term(
            features[member], moment_weights(tile, bodies, blocks, member), x - shift, y, z
        )
        total = [so_far + part for so_far, part in zip(total, term)]
    velocity_ref[...] = rows_of((8, width), total)

    base = lax.axis_index("body") * bodies
    pair_count = pairs.shape[1]
    copy.wait()
    for entry in range(3):
        counts[entry] = 0

    def step_edge(step, carry):
        target = pairs[step % 2, step // 2] - base
        source = pairs[1 - step % 2, step // 2] - base

        @pl.when((target >= 0) & (target < bodies))
        def _():
            inside = (source >= 0) & (source < bodies)
            row = jnp.where(inside, 0, 1)
            slot = jnp.where(inside, source, neighbour_slot(bodies, source))
            place = counts[row]
            codes[pl.ds(row * 2 * pair_count + place, 1), :] = jnp.full(
                (1, 128), target * 16 + slot, jnp.int32
            )
            counts[row] = place + 1
            counts[2] = counts[2] | jnp.where(inside, 0, jnp.left_shift(1, slot))

        return carry

    lax.fori_loop(0, 2 * pair_count, step_edge, 0)
    lane = lax.broadcasted_iota(jnp.int32, (1, 128), 1)
    codes[4 * pair_count : 4 * pair_count + 1, :] = jnp.where(
        lane == 0, counts[0], jnp.where(lane == 1, counts[1], counts[2])
    )


def neighbour_slot(bodies, source):
    upper = (source >= bodies).astype(jnp.int32)
    second = (upper + lax.axis_index("body")) % 2 == 0
    return jnp.where(upper == 1, source - bodies, source + bodies) + jnp.where(second, bodies, 0)


def slot_source(bodies, slot):
    second = (slot >= bodies).astype(jnp.int32)
    upper = (second + lax.axis_index("body")) % 2 == 0
    return slot - second * bodies + jnp.where(upper, bodies, -bodies)


def over_codes(codes, first, count, visit):
    def step_code(step, code):
        following = codes[first + step + 1, 0]
        visit(code // 16, code % 16)
        return following

    lax.fori_loop(0, count, step_code, codes[first, 0])


def group_kernel(
    bodies, codes, tiles_ref, given_ref, own_features, acc_ref, features, weights, spread, surface, points
):
    count, width = tiles_ref.shape[0], acc_ref.shape[2]
    blocks = width // LANES
    rest = (count - 1) * width
    pair_count = codes.shape[0] // 4
    for index in range(1, count):
        tile = tiles_ref[index]
        columns = pl.ds((index - 1) * width, width)
        for member in range(bodies):
            features[member, columns, :] = source_features(*body_points(tile, bodies, blocks, member))
            weights[member, :, columns] = body_weights(tile, blocks, member)
        x, y, z, weight = surface_points(tile, bodies, blocks)
        surface[columns, :] = source_features(x, y, z)
        spread[columns, :] = jnp.broadcast_to(weight, (128, width)).T
    own = tiles_ref[0]
    for member in range(bodies):
        points[member] = rows_of((8, width), body_points(own, bodies, blocks, member))
        features[member, rest:, :] = own_features[member]
        weights[member, :, rest:] = body_weights(own, blocks, member)

    def own_step(member, carry):
        acc_ref[member] = given_ref[member] + influence_sum(
            targets_of(points, member, 0.0), features[member, :rest, :], weights[member, :, :rest]
        )
        shift = (2 * member - (bodies - 1)).astype(full)
        acc_ref[member, 0:1, :] += surface_sum(
            targets_of(points, member, shift), surface[...], spread[...]
        )
        return carry

    lax.fori_loop(0, bodies, own_step, 0)

    def visit(target, source):
        shift = (2 * (target - source)).astype(full)
        acc_ref[target] += influence_sum(
            targets_of(points, target, shift), features[source], weights[source]
        )

    over_codes(codes, 0, codes[4 * pair_count, 0], visit)


def crossing_kernel(
    bodies, codes, first_ref, second_ref, tile_ref, panels_ref, normals_ref, given_ref,
    acc_ref, force_ref, features, weights, points,
):
    count, width = first_ref.shape[0], acc_ref.shape[2]
    blocks = width // LANES
    pair_count = codes.shape[0] // 4
    used = codes[4 * pair_count, 2]
    crossings = codes[4 * pair_count, 1]
    own = tile_ref[...]
    for member in range(bodies):
        points[member] = rows_of((8, width), body_points(own, bodies, blocks, member))
    acc_ref[...] = given_ref[...]
    force_ref[...] = jnp.zeros_like(force_ref)
    for slot in range(2 * bodies):

        @pl.when((jnp.right_shift(used, slot) & 1) == 1)
        def _():
            side = first_ref if slot < bodies else second_ref
            for index in range(count):
                columns = pl.ds(index * width, width)
                tile = side[index]
                member = slot % bodies
                features[slot, columns, :] = source_features(*body_points(tile, bodies, blocks, member))
                weights[slot, :, columns] = body_weights(tile, blocks, member)

    def visit(target, slot):
        source = slot_source(bodies, slot)
        shift = (2 * (target - source)).astype(full)
        acc_ref[target] += influence_sum(
            targets_of(points, target, shift), features[slot], weights[slot]
        )

    over_codes(codes, 2 * pair_count, crossings, visit)
    for member in range(bodies):
        area = panels_ref[3, member : member + 1, :]
        scaled = rows_of(
            (8, width), [normals_ref[axis, member : member + 1, :] * area for axis in range(3)]
        )
        force_ref[member, :, 0:8] = lax.dot_general(
            scaled,
            acc_ref[member],
            (((1,), (1,)), ((), ())),
            precision=lax.Precision.HIGHEST,
            preferred_element_type=full,
        )


def velocity_kernel(
    bodies, tiles_ref, features, given_ref, state_ref, potential_ref, next_ref, potential_hbm, weights, sem
):
    count, width = tiles_ref.shape[0], next_ref.shape[1]
    blocks = width // LANES
    rest = (count - 1) * width
    store = pltpu.make_async_copy(potential_ref, potential_hbm, sem)
    store.start()
    for index in range(1, count):
        tile = tiles_ref[index]
        for member in range(bodies):
            weights[member, :, pl.ds((index - 1) * width, width)] = moment_weights(
                tile, bodies, blocks, member
            )
    own = tiles_ref[0]
    x, y, z, _ = surface_points(own, bodies, blocks)

    def body_step(member, velocity):
        place = x + (bodies - 1 - 2 * member).astype(full)
        term = velocity_term(features[member, :rest, :], weights[member], place, y, z)
        return tuple(so_far + part for so_far, part in zip(velocity, term))

    start = tuple(given_ref[axis : axis + 1, :] for axis in range(3))
    velocity = lax.fori_loop(0, bodies, body_step, start)
    speed_sq = velocity[0] * velocity[0] + velocity[1] * velocity[1] + velocity[2] * velocity[2]
    potential, elevation = state_ref[0:1, :], state_ref[1:2, :]
    next_ref[0:1, :] = potential + time_step * (-gravity * elevation - 0.5 * speed_sq)
    next_ref[1:2, :] = elevation + time_step * velocity[2]
    store.wait()


def finish_kernel(own_ref, first_ref, second_ref, third_ref, next_ref, force_ref, out_ref):
    total = (own_ref[...] + second_ref[...]) + (first_ref[...] + third_ref[...])
    force_ref[...] = total[:, :3, :8]
    out_ref[...] = next_ref[...]


VMEM, SMEM, HBM = pltpu.VMEM, pltpu.SMEM, pltpu.HBM


def call(kernel, operands, results, scratch=(), units=0.0):
    single = len(results) == 1
    out = pl.pallas_call(
        kernel,
        out_shape=[jax.ShapeDtypeStruct(shape, kind) for _, shape, kind in results],
        in_specs=[pl.BlockSpec(memory_space=space) for space, _ in operands],
        out_specs=[pl.BlockSpec(memory_space=space) for space, _, _ in results],
        scratch_shapes=list(scratch),
        compiler_params=pltpu.CompilerParams(vmem_limit_bytes=40 * 1024 * 1024),
        cost_estimate=pl.CostEstimate(
            flops=int(units * 1.2e9), bytes_accessed=1024, transcendentals=0
        ),
    )(*[array for _, array in operands])
    return out[0] if single else out


def rotations(block, axis):
    count = lax.axis_size(axis)
    return [
        lax.ppermute(block, axis, [(i, (i + k) % count) for i in range(count)])
        for k in range(1, count)
    ]


def exchanges(block, axis):
    count = lax.axis_size(axis)
    return [lax.ppermute(block, axis, [(i, i ^ k) for i in range(count)]) for k in range(1, count)]


def on_device(body_panels, body_normals, fs_panels, fs_state, pairs):
    bodies = body_panels.shape[1]
    width = body_panels.shape[2]
    tiles_count = lax.axis_size("surf")
    groups = lax.axis_size("body")
    pair_count = pairs.shape[0]
    semaphore = pltpu.SemaphoreType.DMA
    shifts = call(
        functools.partial(shift_kernel, bodies), [], [(VMEM, (8, 128), full)], units=2.0
    )
    own = call(
        pack_kernel,
        [(VMEM, shifts), (VMEM, body_panels), (VMEM, fs_panels)],
        [(VMEM, (tile_rows(bodies, width), LANES), full)],
    )
    if tiles_count == 4:
        tiles = jnp.stack([own] + exchanges(own, "surf"))
    else:
        everything = lax.all_gather(own, "surf")
        tiles = jnp.concatenate(
            [own[None]]
            + [
                lax.dynamic_index_in_dim(
                    everything, (lax.axis_index("surf") + k) % tiles_count, 0
                )
                for k in range(1, tiles_count)
            ]
        )
    wide = width * tiles_count
    rest = wide - width
    acc_shape = (bodies, 8, width)
    points = VMEM(acc_shape, full)
    partial, velocity, own_features, codes = call(
        functools.partial(own_tile_kernel, bodies),
        [(HBM, pairs.T), (VMEM, own)],
        [
            (VMEM, acc_shape, full),
            (VMEM, (8, width), full),
            (VMEM, (bodies + 1, width, DEPTH), half),
            (VMEM, (code_rows(pair_count), 128), jnp.int32),
        ],
        scratch=(
            VMEM((bodies, 16, width), half),
            VMEM((width, 128), full),
            SMEM((2, pair_count), jnp.int32),
            SMEM((3,), jnp.int32),
            semaphore,
        ),
        units=3.0,
    )
    first, second = [
        lax.ppermute(
            tiles,
            "body",
            [pair for i in range(start, groups - 1, 2) for pair in ((i, i + 1), (i + 1, i))],
        )
        for start in (0, 1)
    ]
    partial, features = call(
        functools.partial(group_kernel, bodies),
        [(VMEM, codes), (VMEM, tiles), (VMEM, partial), (VMEM, own_features)],
        [(VMEM, acc_shape, full), (VMEM, (bodies, wide, DEPTH), half)],
        scratch=(
            VMEM((bodies, 16, wide), half),
            VMEM((rest, 128), full),
            VMEM((rest, DEPTH), half),
            points,
        ),
        units=7.0,
    )
    potential, force = call(
        functools.partial(crossing_kernel, bodies),
        [(VMEM, codes), (VMEM, first), (VMEM, second), (VMEM, own), (VMEM, body_panels),
         (VMEM, body_normals), (VMEM, partial)],
        [(VMEM, acc_shape, full), (VMEM, (bodies, 8, 128), full)],
        scratch=(
            VMEM((2 * bodies, wide, DEPTH), half),
            VMEM((2 * bodies, 16, wide), half),
            points,
        ),
        units=6.0,
    )
    fs_next, own_potential = call(
        functools.partial(velocity_kernel, bodies),
        [(VMEM, tiles), (VMEM, features), (VMEM, velocity), (VMEM, fs_state), (VMEM, potential)],
        [(VMEM, (2, width), full), (HBM, acc_shape, full)],
        scratch=(VMEM((bodies, 16, rest), half), semaphore),
        units=5.0,
    )
    if tiles_count == 4:
        pieces = [force] + rotations(force, "surf")
    else:
        pieces = [lax.psum(force, "surf")] + [jnp.zeros_like(force)] * 3
    total, fs_next = call(
        finish_kernel,
        [(VMEM, piece) for piece in pieces] + [(VMEM, fs_next)],
        [(VMEM, (bodies, 3, 8), full), (VMEM, (2, width), full)],
    )
    return own_potential, total.transpose(0, 2, 1), fs_next


def solution(mesh):
    placed = (
        P(None, "body", "surf"),
        P(None, "body", "surf"),
        P(None, ("body", "surf")),
        P(None, ("body", "surf")),
        P(),
    )
    return jax.shard_map(
        on_device,
        mesh=mesh,
        in_specs=placed,
        out_specs=(P("body", None, "surf"), P("body", None, None), P(None, ("body", "surf"))),
        check_vma=False,
    )
```

```python
import functools

import jax
import jax.numpy as jnp
from jax import lax
from jax.experimental import pallas as pl
from jax.experimental.pallas import tpu as pltpu
from jax.sharding import PartitionSpec as P

soften = 0.01
gravity = 9.81
time_step = 0.2
mid_depth = -1.5
half = jnp.bfloat16
full = jnp.float32
DEPTH = 48


def rows_of(block_shape, rows):
    index = lax.broadcasted_iota(jnp.int32, block_shape, 0)
    block = jnp.zeros(block_shape, full)
    for position, row in enumerate(rows):
        block = jnp.where(index == position, row, block)
    return block


def three_parts(block):
    first = block.astype(half).astype(full)
    rest = block - first
    second = rest.astype(half).astype(full)
    return first, second, rest - second


def source_features(x, y, z):
    norm = x * x + y * y + z * z
    a, b, c = three_parts(rows_of((8, x.shape[1]), (x, y, z, norm, 1.0)))
    return jnp.concatenate([a, b, a, b, c, a], axis=0).astype(half).T


def target_features(x, y, z):
    norm = x * x + y * y + z * z + soften
    a, b, c = three_parts(rows_of((8, x.shape[1]), (-2.0 * x, -2.0 * y, -2.0 * z, 1.0, norm)))
    return jnp.concatenate([a, a, b, b, a, c], axis=0).astype(half)


def two_parts(block):
    first = block.astype(half)
    return first, (block - first.astype(full)).astype(half)


def split_weights(block):
    first = block.astype(half).astype(full)
    return jnp.concatenate([first, block - first], axis=0).astype(half)


def product(left, right):
    return jnp.dot(left, right, preferred_element_type=full)


def weighted_sum(values, weights):
    high, low = two_parts(values)
    both = product(
        jnp.concatenate([weights, weights], axis=1), jnp.concatenate([high, low], axis=0)
    )
    return both[:8] + both[8:]


def influence_sum(targets, sources, weights):
    return weighted_sum(lax.rsqrt(product(sources, targets)), weights)


LANES = 128


def tile_rows(bodies, width):
    return -(-(11 * bodies + 3) * (width // LANES) // 8) * 8


def weight_rows(blocks, member, block):
    start = 8 * (member * blocks + block)
    return slice(start, start + 8)


def entry_row(bodies, blocks, block, entry):
    row = 8 * bodies * blocks + (3 * bodies + 3) * block + entry
    return slice(row, row + 1)


def tile_entry(tile, bodies, blocks, entry):
    return jnp.concatenate(
        [tile[entry_row(bodies, blocks, block, entry), :] for block in range(blocks)], axis=1
    )


def tile_weights(tile, blocks, member):
    return jnp.concatenate(
        [tile[weight_rows(blocks, member, block), :] for block in range(blocks)], axis=1
    )


def body_points(tile, bodies, blocks, member):
    return [tile_entry(tile, bodies, blocks, 3 * member + axis) for axis in range(3)]


def surface_points(tile, bodies, blocks):
    x, y, weight = [tile_entry(tile, bodies, blocks, 3 * bodies + entry) for entry in range(3)]
    return x, y, jnp.full_like(x, -mid_depth), weight


def shift_kernel(bodies, shift_ref):
    base = lax.axis_index("body") * bodies
    row = lax.broadcasted_iota(jnp.int32, shift_ref.shape, 0)
    shift_ref[...] = jnp.where(row < bodies, 2 * (base + row), 2 * base + bodies - 1).astype(full)


def pack_kernel(shift_ref, panels_ref, surface_ref, tile_ref):
    bodies, width = panels_ref.shape[1:]
    blocks = width // LANES
    if tile_ref.shape[0] > (11 * bodies + 3) * blocks:
        tile_ref[...] = jnp.zeros_like(tile_ref)
    for block in range(blocks):
        lanes = slice(block * LANES, (block + 1) * LANES)
        for member in range(bodies):
            row = slice(member, member + 1)
            area = panels_ref[3, row, lanes]
            rows = weight_rows(blocks, member, block)
            for entry in range(8):
                place = rows.start + entry
                tile_ref[place : place + 1, :] = panels_ref[4 + entry, row, lanes] * area
            for axis, shift in enumerate((shift_ref[row, 0:1], 0.0, mid_depth)):
                tile_ref[entry_row(bodies, blocks, block, 3 * member + axis), :] = (
                    panels_ref[axis, row, lanes] - shift
                )
        surface = (
            surface_ref[0:1, lanes] - shift_ref[bodies : bodies + 1, 0:1],
            surface_ref[1:2, lanes],
            surface_ref[2:3, lanes] * surface_ref[3:4, lanes],
        )
        for entry, value in enumerate(surface):
            tile_ref[entry_row(bodies, blocks, block, 3 * bodies + entry), :] = value


def body_weights(tile, blocks, member):
    return split_weights(tile_weights(tile, blocks, member))


def moment_weights(tile, bodies, blocks, member):
    x, y, z = body_points(tile, bodies, blocks, member)
    first = tile_weights(tile, blocks, member)[0:1, :]
    return split_weights(rows_of((8, x.shape[1]), (first, first * x, first * y, first * z)))


def prepare_tile(tile, bodies, blocks, columns, features, weights, spread):
    for member in range(bodies):
        features[member, columns, :] = source_features(*body_points(tile, bodies, blocks, member))
        weights[member, :, columns] = body_weights(tile, blocks, member)
    x, y, z, weight = surface_points(tile, bodies, blocks)
    features[bodies, columns, :] = source_features(x, y, z)
    spread[columns, :] = jnp.broadcast_to(weight, (128, x.shape[1])).T


def surface_sum(targets, sources, spread):
    values = lax.rsqrt(product(sources, targets))
    count, width = values.shape
    sums = []
    for start in range(0, width, 128):
        term = values[:, start : start + 128] * spread
        sums.append(jnp.sum(term.reshape(count // 8, 8, 128), axis=0))
    return jnp.sum(jnp.concatenate(sums, axis=1), axis=0, keepdims=True)


def velocity_term(features, weights, place, y, z):
    inverse = lax.rsqrt(product(features, target_features(place, y, z)))
    moments = weighted_sum(inverse * inverse * inverse, weights)
    return [
        moments[axis + 1 : axis + 2] - at * moments[0:1] for axis, at in enumerate((place, y, z))
    ]


def targets_of(points, member, shift):
    block = points[member]
    return target_features(block[0:1] + shift, block[1:2], block[2:3])


def code_rows(pair_count):
    return 6 * pair_count + 1


def own_tile_kernel(
    bodies, pairs_hbm, tile_ref, acc_ref, velocity_ref, codes,
    features, weights, spread, points, pairs, counts, sem,
):
    width = acc_ref.shape[2]
    blocks = width // LANES
    copy = pltpu.make_async_copy(pairs_hbm, pairs, sem)
    copy.start()
    tile = tile_ref[...]
    prepare_tile(tile, bodies, blocks, pl.ds(0, width), features, weights, spread)
    x, y, z, _ = surface_points(tile, bodies, blocks)
    total = [jnp.zeros((1, width), full)] * 3
    index = lax.broadcasted_iota(jnp.int32, (8, width), 0)
    for member in range(bodies):
        point = body_points(tile, bodies, blocks, member)
        points[member] = rows_of((8, width), point)
        self_part = influence_sum(target_features(*point), features[member], weights[member])
        shift = float(2 * member - (bodies - 1))
        surface_part = surface_sum(
            target_features(point[0] + shift, point[1], point[2]), features[bodies], spread[...]
        )
        acc_ref[member] = self_part + jnp.where(index == 0, surface_part, 0.0)
        term = velocity_term(
            features[member], moment_weights(tile, bodies, blocks, member), x - shift, y, z
        )
        total = [so_far + part for so_far, part in zip(total, term)]
    velocity_ref[...] = rows_of((8, width), total)

    base = lax.axis_index("body") * bodies
    pair_count = pairs.shape[1]
    copy.wait()
    for entry in range(4):
        counts[entry] = 0

    def step_edge(step, carry):
        target = pairs[step % 2, step // 2] - base
        source = pairs[1 - step % 2, step // 2] - base

        @pl.when((target >= 0) & (target < bodies))
        def _():
            inside = (source >= 0) & (source < bodies)
            upper = (source >= bodies).astype(jnp.int32)
            partner = 1 - (upper + lax.axis_index("body")) % 2
            row = jnp.where(inside, 0, 1 + partner)
            slot = jnp.where(
                source < 0, source + bodies, jnp.where(upper == 1, source - bodies, source)
            )
            place = counts[row]
            codes[pl.ds(row * 2 * pair_count + place, 1), :] = jnp.full(
                (1, 128), target * 16 + slot, jnp.int32
            )
            counts[row] = place + 1
            counts[3] = counts[3] | jnp.where(inside, 0, jnp.left_shift(1, partner * bodies + slot))

        return carry

    lax.fori_loop(0, 2 * pair_count, step_edge, 0)
    lane = lax.broadcasted_iota(jnp.int32, (1, 128), 1)
    last = jnp.zeros((1, 128), jnp.int32)
    for entry in range(4):
        last = jnp.where(lane == entry, counts[entry], last)
    codes[6 * pair_count : 6 * pair_count + 1, :] = last
    pair_sums(codes, counts[0], points, features, weights, acc_ref)


def over_codes(codes, first, count, visit):
    def step_code(step, code):
        following = codes[first + step + 1, 0]
        visit(code // 16, code % 16)
        return following

    lax.fori_loop(0, count, step_code, codes[first, 0])


def pair_sums(codes, count, points, features, weights, acc_ref):
    def visit(target, source):
        shift = (2 * (target - source)).astype(full)
        acc_ref[target] += influence_sum(
            targets_of(points, target, shift), features[source], weights[source]
        )

    over_codes(codes, 0, count, visit)


def group_kernel(
    bodies, codes, tiles_ref, given_ref, acc_ref, features, weights, spread, surface, points
):
    count, width = tiles_ref.shape[0], acc_ref.shape[2]
    blocks = width // LANES
    rest = (count - 1) * width
    pair_count = codes.shape[0] // 6
    own = tiles_ref[0]
    for member in range(bodies):
        for index in range(1, count):
            tile = tiles_ref[index]
            columns = pl.ds((index - 1) * width, width)
            features[member, columns, :] = source_features(*body_points(tile, bodies, blocks, member))
            weights[member, :, columns] = body_weights(tile, blocks, member)
        points[member] = rows_of((8, width), body_points(own, bodies, blocks, member))
        acc_ref[member] = given_ref[member] + influence_sum(
            targets_of(points, member, 0.0), features[member], weights[member]
        )
    for index in range(1, count):
        x, y, z, weight = surface_points(tiles_ref[index], bodies, blocks)
        columns = pl.ds((index - 1) * width, width)
        surface[columns, :] = source_features(x, y, z)
        spread[columns, :] = jnp.broadcast_to(weight, (128, width)).T
    for member in range(bodies):
        shift = float(2 * member - (bodies - 1))
        acc_ref[member, 0:1, :] += surface_sum(
            targets_of(points, member, shift), surface[...], spread[...]
        )

    pair_sums(codes, codes[6 * pair_count, 0], points, features, weights, acc_ref)


def partner_sums(bodies, which, codes, side_ref, tile_ref, given_ref, acc_ref, features, weights, points):
    count, width = side_ref.shape[0], acc_ref.shape[2]
    blocks = width // LANES
    pair_count = codes.shape[0] // 6
    crossings = codes[6 * pair_count, 1 + which]
    used = codes[6 * pair_count, 3]
    own = tile_ref[...]
    for member in range(bodies):
        points[member] = rows_of((8, width), body_points(own, bodies, blocks, member))
    acc_ref[...] = given_ref[...]
    for member in range(bodies):

        @pl.when((jnp.right_shift(used, which * bodies + member) & 1) == 1)
        def _():
            for index in range(count):
                columns = pl.ds(index * width, width)
                tile = side_ref[index]
                features[member, columns, :] = source_features(
                    *body_points(tile, bodies, blocks, member)
                )
                weights[member, :, columns] = body_weights(tile, blocks, member)

    upper = (lax.axis_index("body") + which) % 2 == 0
    offset = jnp.where(upper, bodies, -bodies)

    def visit(target, member):
        shift = (2 * (target - member - offset)).astype(full)
        acc_ref[target] += influence_sum(
            targets_of(points, target, shift), features[member], weights[member]
        )

    over_codes(codes, 2 * pair_count * (1 + which), crossings, visit)


def first_partner_kernel(
    bodies, codes, side_ref, tile_ref, given_ref, acc_ref, features, weights, points
):
    partner_sums(
        bodies, 0, codes, side_ref, tile_ref, given_ref, acc_ref, features, weights, points
    )


def second_partner_kernel(
    bodies, codes, side_ref, tile_ref, given_ref, panels_ref, normals_ref,
    acc_ref, force_ref, features, weights, points,
):
    partner_sums(
        bodies, 1, codes, side_ref, tile_ref, given_ref, acc_ref, features, weights, points
    )
    width = acc_ref.shape[2]
    force_ref[...] = jnp.zeros_like(force_ref)
    for member in range(bodies):
        area = panels_ref[3, member : member + 1, :]
        scaled = rows_of(
            (8, width), [normals_ref[axis, member : member + 1, :] * area for axis in range(3)]
        )
        force_ref[member, :, 0:8] = lax.dot_general(
            scaled,
            acc_ref[member],
            (((1,), (1,)), ((), ())),
            precision=lax.Precision.HIGHEST,
            preferred_element_type=full,
        )


def velocity_kernel(
    bodies, tiles_ref, features, given_ref, state_ref, potential_ref, next_ref, potential_hbm, weights, sem
):
    count, width = tiles_ref.shape[0], next_ref.shape[1]
    blocks = width // LANES
    rest = (count - 1) * width
    store = pltpu.make_async_copy(potential_ref, potential_hbm, sem)
    store.start()
    for index in range(1, count):
        tile = tiles_ref[index]
        for member in range(bodies):
            weights[member, :, pl.ds((index - 1) * width, width)] = moment_weights(
                tile, bodies, blocks, member
            )
    own = tiles_ref[0]
    x, y, z, _ = surface_points(own, bodies, blocks)

    velocity = [given_ref[axis : axis + 1, :] for axis in range(3)]
    for member in range(bodies):
        place = x + float(bodies - 1 - 2 * member)
        term = velocity_term(features[member], weights[member], place, y, z)
        velocity = [so_far + part for so_far, part in zip(velocity, term)]
    speed_sq = velocity[0] * velocity[0] + velocity[1] * velocity[1] + velocity[2] * velocity[2]
    potential, elevation = state_ref[0:1, :], state_ref[1:2, :]
    next_ref[0:1, :] = potential + time_step * (-gravity * elevation - 0.5 * speed_sq)
    next_ref[1:2, :] = elevation + time_step * velocity[2]
    store.wait()


def finish_kernel(own_ref, first_ref, second_ref, third_ref, next_ref, force_ref, out_ref):
    total = (own_ref[...] + second_ref[...]) + (first_ref[...] + third_ref[...])
    force_ref[...] = total[:, :3, :8]
    out_ref[...] = next_ref[...]


VMEM, SMEM, HBM = pltpu.VMEM, pltpu.SMEM, pltpu.HBM


def call(kernel, operands, results, scratch=(), units=0.0):
    single = len(results) == 1
    out = pl.pallas_call(
        kernel,
        out_shape=[jax.ShapeDtypeStruct(shape, kind) for _, shape, kind in results],
        in_specs=[pl.BlockSpec(memory_space=space) for space, _ in operands],
        out_specs=[pl.BlockSpec(memory_space=space) for space, _, _ in results],
        scratch_shapes=list(scratch),
        compiler_params=pltpu.CompilerParams(vmem_limit_bytes=40 * 1024 * 1024),
        cost_estimate=pl.CostEstimate(
            flops=int(units * 1.2e9), bytes_accessed=1024, transcendentals=0
        ),
    )(*[array for _, array in operands])
    return out[0] if single else out


def rotations(block, axis):
    count = lax.axis_size(axis)
    return [
        lax.ppermute(block, axis, [(i, (i + k) % count) for i in range(count)])
        for k in range(1, count)
    ]


def exchanges(block, axis):
    count = lax.axis_size(axis)
    return [lax.ppermute(block, axis, [(i, i ^ k) for i in range(count)]) for k in range(1, count)]


def on_device(body_panels, body_normals, fs_panels, fs_state, pairs):
    bodies = body_panels.shape[1]
    width = body_panels.shape[2]
    tiles_count = lax.axis_size("surf")
    groups = lax.axis_size("body")
    pair_count = pairs.shape[0]
    semaphore = pltpu.SemaphoreType.DMA
    shifts = call(
        functools.partial(shift_kernel, bodies), [], [(VMEM, (8, 128), full)], units=2.0
    )
    own = call(
        pack_kernel,
        [(VMEM, shifts), (VMEM, body_panels), (VMEM, fs_panels)],
        [(VMEM, (tile_rows(bodies, width), LANES), full)],
    )
    if tiles_count == 4:
        tiles = jnp.stack([own] + exchanges(own, "surf")[::-1])
    else:
        everything = lax.all_gather(own, "surf")
        tiles = jnp.concatenate(
            [own[None]]
            + [
                lax.dynamic_index_in_dim(
                    everything, (lax.axis_index("surf") + k) % tiles_count, 0
                )
                for k in range(1, tiles_count)
            ]
        )
    wide = width * tiles_count
    rest = wide - width
    acc_shape = (bodies, 8, width)
    points = VMEM(acc_shape, full)
    partial, velocity, codes = call(
        functools.partial(own_tile_kernel, bodies),
        [(HBM, pairs.T), (VMEM, own)],
        [
            (VMEM, acc_shape, full),
            (VMEM, (8, width), full),
            (VMEM, (code_rows(pair_count), 128), jnp.int32),
        ],
        scratch=(
            VMEM((bodies + 1, width, DEPTH), half),
            VMEM((bodies, 16, width), half),
            VMEM((width, 128), full),
            points,
            SMEM((2, pair_count), jnp.int32),
            SMEM((4,), jnp.int32),
            semaphore,
        ),
        units=3.0,
    )
    first, second = [
        lax.ppermute(
            tiles,
            "body",
            [pair for i in range(start, groups - 1, 2) for pair in ((i, i + 1), (i + 1, i))],
        )
        for start in (0, 1)
    ]
    partial, features = call(
        functools.partial(group_kernel, bodies),
        [(VMEM, codes), (VMEM, tiles), (VMEM, partial)],
        [(VMEM, acc_shape, full), (VMEM, (bodies, rest, DEPTH), half)],
        scratch=(
            VMEM((bodies, 16, rest), half),
            VMEM((rest, 128), full),
            VMEM((rest, DEPTH), half),
            points,
        ),
        units=7.0,
    )
    partner_scratch = (
        VMEM((bodies, wide, DEPTH), half),
        VMEM((bodies, 16, wide), half),
        points,
    )
    partial = call(
        functools.partial(first_partner_kernel, bodies),
        [(VMEM, codes), (VMEM, first), (VMEM, own), (VMEM, partial)],
        [(VMEM, acc_shape, full)],
        scratch=partner_scratch,
        units=2.0,
    )
    potential, force = call(
        functools.partial(second_partner_kernel, bodies),
        [(VMEM, codes), (VMEM, second), (VMEM, own), (VMEM, partial), (VMEM, body_panels),
         (VMEM, body_normals)],
        [(VMEM, acc_shape, full), (VMEM, (bodies, 8, 128), full)],
        scratch=partner_scratch,
        units=4.0,
    )
    fs_next, own_potential = call(
        functools.partial(velocity_kernel, bodies),
        [(VMEM, tiles), (VMEM, features), (VMEM, velocity), (VMEM, fs_state), (VMEM, potential)],
        [(VMEM, (2, width), full), (HBM, acc_shape, full)],
        scratch=(VMEM((bodies, 16, rest), half), semaphore),
        units=5.0,
    )
    if tiles_count == 4:
        pieces = [force] + rotations(force, "surf")
    else:
        pieces = [lax.psum(force, "surf")] + [jnp.zeros_like(force)] * 3
    total, fs_next = call(
        finish_kernel,
        [(VMEM, piece) for piece in pieces] + [(VMEM, fs_next)],
        [(VMEM, (bodies, 3, 8), full), (VMEM, (2, width), full)],
    )
    return own_potential, total.transpose(0, 2, 1), fs_next


def solution(mesh):
    placed = (
        P(None, "body", "surf"),
        P(None, "body", "surf"),
        P(None, ("body", "surf")),
        P(None, ("body", "surf")),
        P(),
    )
    return jax.shard_map(
        on_device,
        mesh=mesh,
        in_specs=placed,
        out_specs=(P("body", None, "surf"), P("body", None, None), P(None, ("body", "surf"))),
        check_vma=False,
    )
```

```python
import functools

import jax
import jax.numpy as jnp
from jax import lax
from jax.experimental import pallas as pl
from jax.experimental.pallas import tpu as pltpu
from jax.sharding import PartitionSpec as P

soften = 0.01
gravity = 9.81
time_step = 0.2
mid_depth = -1.5
half = jnp.bfloat16
full = jnp.float32
DEPTH = 48


def rows_of(block_shape, rows):
    index = lax.broadcasted_iota(jnp.int32, block_shape, 0)
    block = jnp.zeros(block_shape, full)
    for position, row in enumerate(rows):
        block = jnp.where(index == position, row, block)
    return block


def three_parts(block):
    first = block.astype(half).astype(full)
    rest = block - first
    second = rest.astype(half).astype(full)
    return first, second, rest - second


def source_features(x, y, z):
    norm = x * x + y * y + z * z
    a, b, c = three_parts(rows_of((8, x.shape[1]), (x, y, z, norm, 1.0)))
    return jnp.concatenate([a, b, a, b, c, a], axis=0).astype(half).T


def target_features(x, y, z):
    norm = x * x + y * y + z * z + soften
    a, b, c = three_parts(rows_of((8, x.shape[1]), (-2.0 * x, -2.0 * y, -2.0 * z, 1.0, norm)))
    return jnp.concatenate([a, a, b, b, a, c], axis=0).astype(half)


def two_parts(block):
    first = block.astype(half)
    return first, (block - first.astype(full)).astype(half)


def split_weights(block):
    first = block.astype(half).astype(full)
    return jnp.concatenate([first, block - first], axis=0).astype(half)


def product(left, right):
    return jnp.dot(left, right, preferred_element_type=full)


def weighted_sum(values, weights):
    high, low = two_parts(values)
    both = product(
        jnp.concatenate([weights, weights], axis=1), jnp.concatenate([high, low], axis=0)
    )
    return both[:8] + both[8:]


def influence_sum(targets, sources, weights):
    return weighted_sum(lax.rsqrt(product(sources, targets)), weights)


LANES = 128


def tile_rows(bodies, width):
    return -(-(11 * bodies + 3) * (width // LANES) // 8) * 8


def weight_rows(blocks, member, block):
    start = 8 * (member * blocks + block)
    return slice(start, start + 8)


def entry_row(bodies, blocks, block, entry):
    row = 8 * bodies * blocks + (3 * bodies + 3) * block + entry
    return slice(row, row + 1)


def tile_entry(tile, bodies, blocks, entry):
    return jnp.concatenate(
        [tile[entry_row(bodies, blocks, block, entry), :] for block in range(blocks)], axis=1
    )


def tile_weights(tile, blocks, member):
    return jnp.concatenate(
        [tile[weight_rows(blocks, member, block), :] for block in range(blocks)], axis=1
    )


def body_points(tile, bodies, blocks, member):
    return [tile_entry(tile, bodies, blocks, 3 * member + axis) for axis in range(3)]


def surface_points(tile, bodies, blocks):
    x, y, weight = [tile_entry(tile, bodies, blocks, 3 * bodies + entry) for entry in range(3)]
    return x, y, jnp.full_like(x, -mid_depth), weight


def shift_kernel(bodies, shift_ref):
    base = lax.axis_index("body") * bodies
    row = lax.broadcasted_iota(jnp.int32, shift_ref.shape, 0)
    shift_ref[...] = jnp.where(row < bodies, 2 * (base + row), 2 * base + bodies - 1).astype(full)


def pack_kernel(shift_ref, panels_ref, surface_ref, tile_ref):
    bodies, width = panels_ref.shape[1:]
    blocks = width // LANES
    if tile_ref.shape[0] > (11 * bodies + 3) * blocks:
        tile_ref[...] = jnp.zeros_like(tile_ref)
    for block in range(blocks):
        lanes = slice(block * LANES, (block + 1) * LANES)
        for member in range(bodies):
            row = slice(member, member + 1)
            area = panels_ref[3, row, lanes]
            rows = weight_rows(blocks, member, block)
            for entry in range(8):
                place = rows.start + entry
                tile_ref[place : place + 1, :] = panels_ref[4 + entry, row, lanes] * area
            for axis, shift in enumerate((shift_ref[row, 0:1], 0.0, mid_depth)):
                tile_ref[entry_row(bodies, blocks, block, 3 * member + axis), :] = (
                    panels_ref[axis, row, lanes] - shift
                )
        surface = (
            surface_ref[0:1, lanes] - shift_ref[bodies : bodies + 1, 0:1],
            surface_ref[1:2, lanes],
            surface_ref[2:3, lanes] * surface_ref[3:4, lanes],
        )
        for entry, value in enumerate(surface):
            tile_ref[entry_row(bodies, blocks, block, 3 * bodies + entry), :] = value


def body_weights(tile, blocks, member):
    return split_weights(tile_weights(tile, blocks, member))


def moment_weights(tile, bodies, blocks, member):
    x, y, z = body_points(tile, bodies, blocks, member)
    first = tile_weights(tile, blocks, member)[0:1, :]
    return split_weights(rows_of((8, x.shape[1]), (first, first * x, first * y, first * z)))


def prepare_tile(tile, bodies, blocks, columns, features, weights, spread):
    for member in range(bodies):
        features[member, columns, :] = source_features(*body_points(tile, bodies, blocks, member))
        weights[member, :, columns] = body_weights(tile, blocks, member)
    x, y, z, weight = surface_points(tile, bodies, blocks)
    features[bodies, columns, :] = source_features(x, y, z)
    spread[columns, :] = jnp.broadcast_to(weight, (128, x.shape[1])).T


def surface_sum(targets, sources, spread):
    values = lax.rsqrt(product(sources, targets))
    count, width = values.shape
    sums = []
    for start in range(0, width, 128):
        term = values[:, start : start + 128] * spread
        sums.append(jnp.sum(term.reshape(count // 8, 8, 128), axis=0))
    return jnp.sum(jnp.concatenate(sums, axis=1), axis=0, keepdims=True)


def velocity_term(features, weights, place, y, z):
    inverse = lax.rsqrt(product(features, target_features(place, y, z)))
    moments = weighted_sum(inverse * inverse * inverse, weights)
    return [
        moments[axis + 1 : axis + 2] - at * moments[0:1] for axis, at in enumerate((place, y, z))
    ]


def targets_of(points, member, shift):
    block = points[member]
    return target_features(block[0:1] + shift, block[1:2], block[2:3])


def code_rows(pair_count):
    return 6 * pair_count + 1


def own_tile_kernel(
    bodies, pairs_hbm, tile_ref, acc_ref, velocity_ref, codes,
    features, weights, spread, points, pairs, counts, sem,
):
    width = acc_ref.shape[2]
    blocks = width // LANES
    copy = pltpu.make_async_copy(pairs_hbm, pairs, sem)
    copy.start()
    tile = tile_ref[...]
    prepare_tile(tile, bodies, blocks, pl.ds(0, width), features, weights, spread)
    x, y, z, _ = surface_points(tile, bodies, blocks)
    total = [jnp.zeros((1, width), full)] * 3
    index = lax.broadcasted_iota(jnp.int32, (8, width), 0)
    for member in range(bodies):
        point = body_points(tile, bodies, blocks, member)
        points[member] = rows_of((8, width), point)
        self_part = influence_sum(target_features(*point), features[member], weights[member])
        shift = float(2 * member - (bodies - 1))
        surface_part = surface_sum(
            target_features(point[0] + shift, point[1], point[2]), features[bodies], spread[...]
        )
        acc_ref[member] = self_part + jnp.where(index == 0, surface_part, 0.0)
        term = velocity_term(
            features[member], moment_weights(tile, bodies, blocks, member), x - shift, y, z
        )
        total = [so_far + part for so_far, part in zip(total, term)]
    velocity_ref[...] = rows_of((8, width), total)

    base = lax.axis_index("body") * bodies
    pair_count = pairs.shape[1]
    copy.wait()
    for entry in range(4):
        counts[entry] = 0

    def list_pair(step, carry):
        low, high = pairs[0, step] - base, pairs[1, step] - base

        @pl.when((high >= 0) & (low < bodies) & ((low >= 0) | (high < bodies)))
        def _():
            inside = (low >= 0) & (high < bodies)
            upper = (low >= 0).astype(jnp.int32)
            target = jnp.where(upper == 1, low, high)
            source = jnp.where(upper == 1, high - jnp.where(inside, 0, bodies), low + bodies)
            partner = 1 - (upper + lax.axis_index("body")) % 2
            row = jnp.where(inside, 0, 1 + partner)
            place = counts[row]
            codes[pl.ds(row * 2 * pair_count + place, 1), :] = jnp.full(
                (1, 128), target * 16 + source, jnp.int32
            )
            counts[row] = place + 1
            counts[3] = counts[3] | jnp.where(
                inside, 0, jnp.left_shift(1, partner * bodies + source)
            )

        return carry

    lax.fori_loop(0, pair_count, list_pair, 0)
    lane = lax.broadcasted_iota(jnp.int32, (1, 128), 1)
    last = jnp.zeros((1, 128), jnp.int32)
    for entry in range(4):
        last = jnp.where(lane == entry, counts[entry], last)
    codes[6 * pair_count : 6 * pair_count + 1, :] = last
    pair_sums(codes, counts[0], points, features, weights, acc_ref)


def over_codes(codes, first, count, visit):
    def step_code(step, code):
        following = codes[first + step + 1, 0]
        visit(code // 16, code % 16)
        return following

    lax.fori_loop(0, count, step_code, codes[first, 0])


def pair_sums(codes, count, points, features, weights, acc_ref):
    def visit(low, high):
        shift = (2 * (low - high)).astype(full)
        to_low = influence_sum(targets_of(points, low, shift), features[high], weights[high])
        to_high = influence_sum(targets_of(points, high, -shift), features[low], weights[low])
        acc_ref[low] += to_low
        acc_ref[high] += to_high

    over_codes(codes, 0, count, visit)


def group_kernel(
    bodies, codes, tiles_ref, given_ref, acc_ref, features, weights, spread, surface, points
):
    count, width = tiles_ref.shape[0], acc_ref.shape[2]
    blocks = width // LANES
    rest = (count - 1) * width
    pair_count = codes.shape[0] // 6
    own = tiles_ref[0]
    for member in range(bodies):
        for index in range(1, count):
            tile = tiles_ref[index]
            columns = pl.ds((index - 1) * width, width)
            features[member, columns, :] = source_features(*body_points(tile, bodies, blocks, member))
            weights[member, :, columns] = body_weights(tile, blocks, member)
        points[member] = rows_of((8, width), body_points(own, bodies, blocks, member))
        acc_ref[member] = given_ref[member] + influence_sum(
            targets_of(points, member, 0.0), features[member], weights[member]
        )
    for index in range(1, count):
        x, y, z, weight = surface_points(tiles_ref[index], bodies, blocks)
        columns = pl.ds((index - 1) * width, width)
        surface[columns, :] = source_features(x, y, z)
        spread[columns, :] = jnp.broadcast_to(weight, (128, width)).T
    for member in range(bodies):
        shift = float(2 * member - (bodies - 1))
        acc_ref[member, 0:1, :] += surface_sum(
            targets_of(points, member, shift), surface[...], spread[...]
        )

    pair_sums(codes, codes[6 * pair_count, 0], points, features, weights, acc_ref)


def partner_sums(bodies, which, codes, side_ref, tile_ref, given_ref, acc_ref, features, weights, points):
    count, width = side_ref.shape[0], acc_ref.shape[2]
    blocks = width // LANES
    pair_count = codes.shape[0] // 6
    crossings = codes[6 * pair_count, 1 + which]
    used = codes[6 * pair_count, 3]
    own = tile_ref[...]
    for member in range(bodies):
        points[member] = rows_of((8, width), body_points(own, bodies, blocks, member))
    acc_ref[...] = given_ref[...]
    for member in range(bodies):

        @pl.when((jnp.right_shift(used, which * bodies + member) & 1) == 1)
        def _():
            for index in range(count):
                columns = pl.ds(index * width, width)
                tile = side_ref[index]
                features[member, columns, :] = source_features(
                    *body_points(tile, bodies, blocks, member)
                )
                weights[member, :, columns] = body_weights(tile, blocks, member)

    upper = (lax.axis_index("body") + which) % 2 == 0
    offset = jnp.where(upper, bodies, -bodies)

    def visit(target, member):
        shift = (2 * (target - member - offset)).astype(full)
        acc_ref[target] += influence_sum(
            targets_of(points, target, shift), features[member], weights[member]
        )

    over_codes(codes, 2 * pair_count * (1 + which), crossings, visit)


def first_partner_kernel(
    bodies, codes, side_ref, tile_ref, given_ref, acc_ref, features, weights, points
):
    partner_sums(
        bodies, 0, codes, side_ref, tile_ref, given_ref, acc_ref, features, weights, points
    )


def second_partner_kernel(
    bodies, codes, side_ref, tile_ref, given_ref, panels_ref, normals_ref,
    acc_ref, force_ref, features, weights, points,
):
    partner_sums(
        bodies, 1, codes, side_ref, tile_ref, given_ref, acc_ref, features, weights, points
    )
    width = acc_ref.shape[2]
    force_ref[...] = jnp.zeros_like(force_ref)
    for member in range(bodies):
        area = panels_ref[3, member : member + 1, :]
        scaled = rows_of(
            (8, width), [normals_ref[axis, member : member + 1, :] * area for axis in range(3)]
        )
        force_ref[member, :, 0:8] = lax.dot_general(
            scaled,
            acc_ref[member],
            (((1,), (1,)), ((), ())),
            precision=lax.Precision.HIGHEST,
            preferred_element_type=full,
        )


def velocity_kernel(
    bodies, tiles_ref, features, given_ref, state_ref, potential_ref, next_ref, potential_hbm, weights, sem
):
    count, width = tiles_ref.shape[0], next_ref.shape[1]
    blocks = width // LANES
    rest = (count - 1) * width
    store = pltpu.make_async_copy(potential_ref, potential_hbm, sem)
    store.start()
    for index in range(1, count):
        tile = tiles_ref[index]
        for member in range(bodies):
            weights[member, :, pl.ds((index - 1) * width, width)] = moment_weights(
                tile, bodies, blocks, member
            )
    own = tiles_ref[0]
    x, y, z, _ = surface_points(own, bodies, blocks)

    velocity = [given_ref[axis : axis + 1, :] for axis in range(3)]
    for member in range(bodies):
        place = x + float(bodies - 1 - 2 * member)
        term = velocity_term(features[member], weights[member], place, y, z)
        velocity = [so_far + part for so_far, part in zip(velocity, term)]
    speed_sq = velocity[0] * velocity[0] + velocity[1] * velocity[1] + velocity[2] * velocity[2]
    potential, elevation = state_ref[0:1, :], state_ref[1:2, :]
    next_ref[0:1, :] = potential + time_step * (-gravity * elevation - 0.5 * speed_sq)
    next_ref[1:2, :] = elevation + time_step * velocity[2]
    store.wait()


def finish_kernel(own_ref, first_ref, second_ref, third_ref, next_ref, force_ref, out_ref):
    total = (own_ref[...] + second_ref[...]) + (first_ref[...] + third_ref[...])
    force_ref[...] = total[:, :3, :8]
    out_ref[...] = next_ref[...]


VMEM, SMEM, HBM = pltpu.VMEM, pltpu.SMEM, pltpu.HBM


def call(kernel, operands, results, scratch=(), units=0.0):
    single = len(results) == 1
    out = pl.pallas_call(
        kernel,
        out_shape=[jax.ShapeDtypeStruct(shape, kind) for _, shape, kind in results],
        in_specs=[pl.BlockSpec(memory_space=space) for space, _ in operands],
        out_specs=[pl.BlockSpec(memory_space=space) for space, _, _ in results],
        scratch_shapes=list(scratch),
        compiler_params=pltpu.CompilerParams(vmem_limit_bytes=40 * 1024 * 1024),
        cost_estimate=pl.CostEstimate(
            flops=int(units * 1.2e9), bytes_accessed=1024, transcendentals=0
        ),
    )(*[array for _, array in operands])
    return out[0] if single else out


def rotations(block, axis):
    count = lax.axis_size(axis)
    return [
        lax.ppermute(block, axis, [(i, (i + k) % count) for i in range(count)])
        for k in range(1, count)
    ]


def exchanges(block, axis):
    count = lax.axis_size(axis)
    return [lax.ppermute(block, axis, [(i, i ^ k) for i in range(count)]) for k in range(1, count)]


def on_device(body_panels, body_normals, fs_panels, fs_state, pairs):
    bodies = body_panels.shape[1]
    width = body_panels.shape[2]
    tiles_count = lax.axis_size("surf")
    groups = lax.axis_size("body")
    pair_count = pairs.shape[0]
    semaphore = pltpu.SemaphoreType.DMA
    shifts = call(
        functools.partial(shift_kernel, bodies), [], [(VMEM, (8, 128), full)], units=2.0
    )
    own = call(
        pack_kernel,
        [(VMEM, shifts), (VMEM, body_panels), (VMEM, fs_panels)],
        [(VMEM, (tile_rows(bodies, width), LANES), full)],
    )
    if tiles_count == 4:
        tiles = jnp.stack([own] + exchanges(own, "surf")[::-1])
    else:
        everything = lax.all_gather(own, "surf")
        tiles = jnp.concatenate(
            [own[None]]
            + [
                lax.dynamic_index_in_dim(
                    everything, (lax.axis_index("surf") + k) % tiles_count, 0
                )
                for k in range(1, tiles_count)
            ]
        )
    wide = width * tiles_count
    rest = wide - width
    acc_shape = (bodies, 8, width)
    points = VMEM(acc_shape, full)
    partial, velocity, codes = call(
        functools.partial(own_tile_kernel, bodies),
        [(HBM, pairs.T), (VMEM, own)],
        [
            (VMEM, acc_shape, full),
            (VMEM, (8, width), full),
            (VMEM, (code_rows(pair_count), 128), jnp.int32),
        ],
        scratch=(
            VMEM((bodies + 1, width, DEPTH), half),
            VMEM((bodies, 16, width), half),
            VMEM((width, 128), full),
            points,
            SMEM((2, pair_count), jnp.int32),
            SMEM((4,), jnp.int32),
            semaphore,
        ),
        units=3.0,
    )
    first, second = [
        lax.ppermute(
            tiles,
            "body",
            [pair for i in range(start, groups - 1, 2) for pair in ((i, i + 1), (i + 1, i))],
        )
        for start in (0, 1)
    ]
    partial, features = call(
        functools.partial(group_kernel, bodies),
        [(VMEM, codes), (VMEM, tiles), (VMEM, partial)],
        [(VMEM, acc_shape, full), (VMEM, (bodies, rest, DEPTH), half)],
        scratch=(
            VMEM((bodies, 16, rest), half),
            VMEM((rest, 128), full),
            VMEM((rest, DEPTH), half),
            points,
        ),
        units=7.0,
    )
    partner_scratch = (
        VMEM((bodies, wide, DEPTH), half),
        VMEM((bodies, 16, wide), half),
        points,
    )
    partial = call(
        functools.partial(first_partner_kernel, bodies),
        [(VMEM, codes), (VMEM, first), (VMEM, own), (VMEM, partial)],
        [(VMEM, acc_shape, full)],
        scratch=partner_scratch,
        units=2.0,
    )
    potential, force = call(
        functools.partial(second_partner_kernel, bodies),
        [(VMEM, codes), (VMEM, second), (VMEM, own), (VMEM, partial), (VMEM, body_panels),
         (VMEM, body_normals)],
        [(VMEM, acc_shape, full), (VMEM, (bodies, 8, 128), full)],
        scratch=partner_scratch,
        units=4.0,
    )
    fs_next, own_potential = call(
        functools.partial(velocity_kernel, bodies),
        [(VMEM, tiles), (VMEM, features), (VMEM, velocity), (VMEM, fs_state), (VMEM, potential)],
        [(VMEM, (2, width), full), (HBM, acc_shape, full)],
        scratch=(VMEM((bodies, 16, rest), half), semaphore),
        units=5.0,
    )
    if tiles_count == 4:
        pieces = [force] + rotations(force, "surf")
    else:
        pieces = [lax.psum(force, "surf")] + [jnp.zeros_like(force)] * 3
    total, fs_next = call(
        finish_kernel,
        [(VMEM, piece) for piece in pieces] + [(VMEM, fs_next)],
        [(VMEM, (bodies, 3, 8), full), (VMEM, (2, width), full)],
    )
    return own_potential, total.transpose(0, 2, 1), fs_next


def solution(mesh):
    placed = (
        P(None, "body", "surf"),
        P(None, "body", "surf"),
        P(None, ("body", "surf")),
        P(None, ("body", "surf")),
        P(),
    )
    return jax.shard_map(
        on_device,
        mesh=mesh,
        in_specs=placed,
        out_specs=(P("body", None, "surf"), P("body", None, None), P(None, ("body", "surf"))),
        check_vma=False,
    )
```

```python
import functools

import jax
import jax.numpy as jnp
from jax import lax
from jax.experimental import pallas as pl
from jax.experimental.pallas import tpu as pltpu
from jax.sharding import PartitionSpec as P

soften = 0.01
gravity = 9.81
time_step = 0.2
mid_depth = -1.5
half = jnp.bfloat16
full = jnp.float32
DEPTH = 48


def rows_of(block_shape, rows):
    index = lax.broadcasted_iota(jnp.int32, block_shape, 0)
    block = jnp.zeros(block_shape, full)
    for position, row in enumerate(rows):
        block = jnp.where(index == position, row, block)
    return block


def three_parts(block):
    first = block.astype(half).astype(full)
    rest = block - first
    second = rest.astype(half).astype(full)
    return first, second, rest - second


def source_features(x, y, z):
    norm = x * x + y * y + z * z
    a, b, c = three_parts(rows_of((8, x.shape[1]), (x, y, z, norm, 1.0)))
    return jnp.concatenate([a, b, a, b, c, a], axis=0).astype(half).T


def target_features(x, y, z):
    norm = x * x + y * y + z * z + soften
    a, b, c = three_parts(rows_of((8, x.shape[1]), (-2.0 * x, -2.0 * y, -2.0 * z, 1.0, norm)))
    return jnp.concatenate([a, a, b, b, a, c], axis=0).astype(half)


def two_parts(block):
    first = block.astype(half)
    return first, (block - first.astype(full)).astype(half)


def split_weights(block):
    first = block.astype(half).astype(full)
    return jnp.concatenate([first, block - first], axis=0).astype(half)


def product(left, right):
    return jnp.dot(left, right, preferred_element_type=full)


def weighted_sum(values, weights):
    high, low = two_parts(values)
    both = product(
        jnp.concatenate([weights, weights], axis=1), jnp.concatenate([high, low], axis=0)
    )
    return both[:8] + both[8:]


def influence_sum(targets, sources, weights):
    return weighted_sum(lax.rsqrt(product(sources, targets)), weights)


LANES = 128


def tile_rows(bodies, width):
    return -(-(11 * bodies + 3) * (width // LANES) // 8) * 8


def weight_rows(blocks, member, block):
    start = 8 * (member * blocks + block)
    return slice(start, start + 8)


def entry_row(bodies, blocks, block, entry):
    row = 8 * bodies * blocks + (3 * bodies + 3) * block + entry
    return slice(row, row + 1)


def tile_entry(tile, bodies, blocks, entry):
    return jnp.concatenate(
        [tile[entry_row(bodies, blocks, block, entry), :] for block in range(blocks)], axis=1
    )


def tile_weights(tile, blocks, member):
    return jnp.concatenate(
        [tile[weight_rows(blocks, member, block), :] for block in range(blocks)], axis=1
    )


def body_points(tile, bodies, blocks, member):
    return [tile_entry(tile, bodies, blocks, 3 * member + axis) for axis in range(3)]


def surface_points(tile, bodies, blocks):
    x, y, weight = [tile_entry(tile, bodies, blocks, 3 * bodies + entry) for entry in range(3)]
    return x, y, jnp.full_like(x, -mid_depth), weight


def shift_kernel(bodies, shift_ref):
    base = lax.axis_index("body") * bodies
    row = lax.broadcasted_iota(jnp.int32, shift_ref.shape, 0)
    shift_ref[...] = jnp.where(row < bodies, 2 * (base + row), 2 * base + bodies - 1).astype(full)


def pack_kernel(shift_ref, panels_ref, surface_ref, tile_ref):
    bodies, width = panels_ref.shape[1:]
    blocks = width // LANES
    if tile_ref.shape[0] > (11 * bodies + 3) * blocks:
        tile_ref[...] = jnp.zeros_like(tile_ref)
    for block in range(blocks):
        lanes = slice(block * LANES, (block + 1) * LANES)
        for member in range(bodies):
            row = slice(member, member + 1)
            area = panels_ref[3, row, lanes]
            rows = weight_rows(blocks, member, block)
            for entry in range(8):
                place = rows.start + entry
                tile_ref[place : place + 1, :] = panels_ref[4 + entry, row, lanes] * area
            for axis, shift in enumerate((shift_ref[row, 0:1], 0.0, mid_depth)):
                tile_ref[entry_row(bodies, blocks, block, 3 * member + axis), :] = (
                    panels_ref[axis, row, lanes] - shift
                )
        surface = (
            surface_ref[0:1, lanes] - shift_ref[bodies : bodies + 1, 0:1],
            surface_ref[1:2, lanes],
            surface_ref[2:3, lanes] * surface_ref[3:4, lanes],
        )
        for entry, value in enumerate(surface):
            tile_ref[entry_row(bodies, blocks, block, 3 * bodies + entry), :] = value


def body_weights(tile, blocks, member):
    return split_weights(tile_weights(tile, blocks, member))


def moment_weights(tile, bodies, blocks, member):
    x, y, z = body_points(tile, bodies, blocks, member)
    first = tile_weights(tile, blocks, member)[0:1, :]
    return split_weights(rows_of((8, x.shape[1]), (first, first * x, first * y, first * z)))


def prepare_tile(tile, bodies, blocks, columns, features, weights, spread):
    for member in range(bodies):
        features[member, columns, :] = source_features(*body_points(tile, bodies, blocks, member))
        weights[member, :, columns] = body_weights(tile, blocks, member)
    x, y, z, weight = surface_points(tile, bodies, blocks)
    features[bodies, columns, :] = source_features(x, y, z)
    spread[columns, :] = jnp.broadcast_to(weight, (128, x.shape[1])).T


def surface_sum(targets, sources, spread):
    values = lax.rsqrt(product(sources, targets))
    count, width = values.shape
    sums = []
    for start in range(0, width, 128):
        term = values[:, start : start + 128] * spread
        sums.append(jnp.sum(term.reshape(count // 8, 8, 128), axis=0))
    return jnp.sum(jnp.concatenate(sums, axis=1), axis=0, keepdims=True)


def velocity_term(features, weights, place, y, z):
    inverse = lax.rsqrt(product(features, target_features(place, y, z)))
    moments = weighted_sum(inverse * inverse * inverse, weights)
    return [
        moments[axis + 1 : axis + 2] - at * moments[0:1] for axis, at in enumerate((place, y, z))
    ]


def targets_of(points, member, shift):
    block = points[member]
    return target_features(block[0:1] + shift, block[1:2], block[2:3])


def code_rows(pair_count):
    return 6 * pair_count + 1


def own_tile_kernel(
    bodies, pairs_hbm, tile_ref, panels_ref, normals_ref, acc_ref, velocity_ref, codes, scaled_ref,
    features, weights, spread, points, pairs, counts, sem,
):
    width = acc_ref.shape[2]
    blocks = width // LANES
    copy = pltpu.make_async_copy(pairs_hbm, pairs, sem)
    copy.start()
    tile = tile_ref[...]
    prepare_tile(tile, bodies, blocks, pl.ds(0, width), features, weights, spread)
    x, y, z, _ = surface_points(tile, bodies, blocks)
    total = [jnp.zeros((1, width), full)] * 3
    index = lax.broadcasted_iota(jnp.int32, (8, width), 0)
    for member in range(bodies):
        point = body_points(tile, bodies, blocks, member)
        points[member] = rows_of((8, width), point)
        self_part = influence_sum(target_features(*point), features[member], weights[member])
        shift = float(2 * member - (bodies - 1))
        surface_part = surface_sum(
            target_features(point[0] + shift, point[1], point[2]), features[bodies], spread[...]
        )
        acc_ref[member] = self_part + jnp.where(index == 0, surface_part, 0.0)
        term = velocity_term(
            features[member], moment_weights(tile, bodies, blocks, member), x - shift, y, z
        )
        total = [so_far + part for so_far, part in zip(total, term)]
    velocity_ref[...] = rows_of((8, width), total)
    for member in range(bodies):
        area = panels_ref[3, member : member + 1, :]
        scaled_ref[member] = rows_of(
            (8, width), [normals_ref[axis, member : member + 1, :] * area for axis in range(3)]
        )

    base = lax.axis_index("body") * bodies
    pair_count = pairs.shape[1]
    copy.wait()
    for entry in range(4):
        counts[entry] = 0

    def list_pair(step, carry):
        low, high = pairs[0, step] - base, pairs[1, step] - base

        @pl.when((high >= 0) & (low < bodies) & ((low >= 0) | (high < bodies)))
        def _():
            inside = (low >= 0) & (high < bodies)
            upper = (low >= 0).astype(jnp.int32)
            target = jnp.where(upper == 1, low, high)
            source = jnp.where(upper == 1, high - jnp.where(inside, 0, bodies), low + bodies)
            partner = 1 - (upper + lax.axis_index("body")) % 2
            row = jnp.where(inside, 0, 1 + partner)
            place = counts[row]
            codes[pl.ds(row * 2 * pair_count + place, 1), :] = jnp.full(
                (1, 128), target * 16 + source, jnp.int32
            )
            counts[row] = place + 1
            counts[3] = counts[3] | jnp.where(
                inside, 0, jnp.left_shift(1, partner * bodies + source)
            )

        return carry

    lax.fori_loop(0, pair_count, list_pair, 0)
    lane = lax.broadcasted_iota(jnp.int32, (1, 128), 1)
    last = jnp.zeros((1, 128), jnp.int32)
    for entry in range(4):
        last = jnp.where(lane == entry, counts[entry], last)
    codes[6 * pair_count : 6 * pair_count + 1, :] = last
    pair_sums(codes, counts[0], points, features, weights, acc_ref)


def over_codes(codes, first, count, visit):
    def step_code(step, code):
        following = codes[first + step + 1, 0]
        visit(code // 16, code % 16)
        return following

    lax.fori_loop(0, count, step_code, codes[first, 0])


def pair_sums(codes, count, points, features, weights, acc_ref):
    def visit(low, high):
        shift = (2 * (low - high)).astype(full)
        to_low = influence_sum(targets_of(points, low, shift), features[high], weights[high])
        to_high = influence_sum(targets_of(points, high, -shift), features[low], weights[low])
        acc_ref[low] += to_low
        acc_ref[high] += to_high

    over_codes(codes, 0, count, visit)


def group_kernel(
    bodies, codes, tiles_ref, given_ref, acc_ref, features, weights, spread, surface, points
):
    count, width = tiles_ref.shape[0], acc_ref.shape[2]
    blocks = width // LANES
    rest = (count - 1) * width
    pair_count = codes.shape[0] // 6
    own = tiles_ref[0]
    for member in range(bodies):
        for index in range(1, count):
            tile = tiles_ref[index]
            columns = pl.ds((index - 1) * width, width)
            features[member, columns, :] = source_features(*body_points(tile, bodies, blocks, member))
            weights[member, :, columns] = body_weights(tile, blocks, member)
        points[member] = rows_of((8, width), body_points(own, bodies, blocks, member))
        acc_ref[member] = given_ref[member] + influence_sum(
            targets_of(points, member, 0.0), features[member], weights[member]
        )
    for index in range(1, count):
        x, y, z, weight = surface_points(tiles_ref[index], bodies, blocks)
        columns = pl.ds((index - 1) * width, width)
        surface[columns, :] = source_features(x, y, z)
        spread[columns, :] = jnp.broadcast_to(weight, (128, width)).T
    for member in range(bodies):
        shift = float(2 * member - (bodies - 1))
        acc_ref[member, 0:1, :] += surface_sum(
            targets_of(points, member, shift), surface[...], spread[...]
        )

    pair_sums(codes, codes[6 * pair_count, 0], points, features, weights, acc_ref)


def partner_sums(bodies, which, codes, side_ref, tile_ref, given_ref, acc_ref, features, weights, points):
    count, width = side_ref.shape[0], acc_ref.shape[2]
    blocks = width // LANES
    pair_count = codes.shape[0] // 6
    crossings = codes[6 * pair_count, 1 + which]
    used = codes[6 * pair_count, 3]
    own = tile_ref[...]
    for member in range(bodies):
        points[member] = rows_of((8, width), body_points(own, bodies, blocks, member))
    acc_ref[...] = given_ref[...]
    for member in range(bodies):

        @pl.when((jnp.right_shift(used, which * bodies + member) & 1) == 1)
        def _():
            for index in range(count):
                columns = pl.ds(index * width, width)
                tile = side_ref[index]
                features[member, columns, :] = source_features(
                    *body_points(tile, bodies, blocks, member)
                )
                weights[member, :, columns] = body_weights(tile, blocks, member)

    upper = (lax.axis_index("body") + which) % 2 == 0
    offset = jnp.where(upper, bodies, -bodies)

    def visit(target, member):
        shift = (2 * (target - member - offset)).astype(full)
        acc_ref[target] += influence_sum(
            targets_of(points, target, shift), features[member], weights[member]
        )

    over_codes(codes, 2 * pair_count * (1 + which), crossings, visit)


def first_partner_kernel(
    bodies, codes, side_ref, tile_ref, given_ref, acc_ref, features, weights, points
):
    partner_sums(
        bodies, 0, codes, side_ref, tile_ref, given_ref, acc_ref, features, weights, points
    )


def second_partner_kernel(
    bodies, codes, side_ref, tile_ref, given_ref, scaled_ref,
    acc_ref, force_ref, features, weights, points,
):
    partner_sums(
        bodies, 1, codes, side_ref, tile_ref, given_ref, acc_ref, features, weights, points
    )
    force_ref[...] = jnp.zeros_like(force_ref)
    for member in range(bodies):
        force_ref[member, :, 0:8] = lax.dot_general(
            scaled_ref[member],
            acc_ref[member],
            (((1,), (1,)), ((), ())),
            precision=lax.Precision.HIGHEST,
            preferred_element_type=full,
        )


def velocity_kernel(
    bodies, tiles_ref, features, given_ref, state_ref, potential_ref, next_ref, potential_hbm, weights, sem
):
    count, width = tiles_ref.shape[0], next_ref.shape[1]
    blocks = width // LANES
    rest = (count - 1) * width
    store = pltpu.make_async_copy(potential_ref, potential_hbm, sem)
    store.start()
    for index in range(1, count):
        tile = tiles_ref[index]
        for member in range(bodies):
            weights[member, :, pl.ds((index - 1) * width, width)] = moment_weights(
                tile, bodies, blocks, member
            )
    own = tiles_ref[0]
    x, y, z, _ = surface_points(own, bodies, blocks)

    velocity = [given_ref[axis : axis + 1, :] for axis in range(3)]
    for member in range(bodies):
        place = x + float(bodies - 1 - 2 * member)
        term = velocity_term(features[member], weights[member], place, y, z)
        velocity = [so_far + part for so_far, part in zip(velocity, term)]
    speed_sq = velocity[0] * velocity[0] + velocity[1] * velocity[1] + velocity[2] * velocity[2]
    potential, elevation = state_ref[0:1, :], state_ref[1:2, :]
    next_ref[0:1, :] = potential + time_step * (-gravity * elevation - 0.5 * speed_sq)
    next_ref[1:2, :] = elevation + time_step * velocity[2]
    store.wait()


def finish_kernel(own_ref, first_ref, second_ref, third_ref, next_ref, force_ref, out_ref):
    total = (own_ref[...] + second_ref[...]) + (first_ref[...] + third_ref[...])
    force_ref[...] = total[:, :3, :8]
    out_ref[...] = next_ref[...]


VMEM, SMEM, HBM = pltpu.VMEM, pltpu.SMEM, pltpu.HBM


def call(kernel, operands, results, scratch=(), units=0.0):
    single = len(results) == 1
    out = pl.pallas_call(
        kernel,
        out_shape=[jax.ShapeDtypeStruct(shape, kind) for _, shape, kind in results],
        in_specs=[pl.BlockSpec(memory_space=space) for space, _ in operands],
        out_specs=[pl.BlockSpec(memory_space=space) for space, _, _ in results],
        scratch_shapes=list(scratch),
        compiler_params=pltpu.CompilerParams(vmem_limit_bytes=40 * 1024 * 1024),
        cost_estimate=pl.CostEstimate(
            flops=int(units * 1.2e9), bytes_accessed=1024, transcendentals=0
        ),
    )(*[array for _, array in operands])
    return out[0] if single else out


def rotations(block, axis):
    count = lax.axis_size(axis)
    return [
        lax.ppermute(block, axis, [(i, (i + k) % count) for i in range(count)])
        for k in range(1, count)
    ]


def exchanges(block, axis):
    count = lax.axis_size(axis)
    return [lax.ppermute(block, axis, [(i, i ^ k) for i in range(count)]) for k in range(1, count)]


def on_device(body_panels, body_normals, fs_panels, fs_state, pairs):
    bodies = body_panels.shape[1]
    width = body_panels.shape[2]
    tiles_count = lax.axis_size("surf")
    groups = lax.axis_size("body")
    pair_count = pairs.shape[0]
    semaphore = pltpu.SemaphoreType.DMA
    shifts = call(
        functools.partial(shift_kernel, bodies), [], [(VMEM, (8, 128), full)], units=2.0
    )
    own = call(
        pack_kernel,
        [(VMEM, shifts), (VMEM, body_panels), (VMEM, fs_panels)],
        [(VMEM, (tile_rows(bodies, width), LANES), full)],
    )
    if tiles_count == 4:
        tiles = jnp.stack([own] + exchanges(own, "surf")[::-1])
    else:
        everything = lax.all_gather(own, "surf")
        tiles = jnp.concatenate(
            [own[None]]
            + [
                lax.dynamic_index_in_dim(
                    everything, (lax.axis_index("surf") + k) % tiles_count, 0
                )
                for k in range(1, tiles_count)
            ]
        )
    wide = width * tiles_count
    rest = wide - width
    acc_shape = (bodies, 8, width)
    points = VMEM(acc_shape, full)
    partial, velocity, codes, scaled = call(
        functools.partial(own_tile_kernel, bodies),
        [(HBM, pairs.T), (VMEM, own), (VMEM, body_panels), (VMEM, body_normals)],
        [
            (VMEM, acc_shape, full),
            (VMEM, (8, width), full),
            (VMEM, (code_rows(pair_count), 128), jnp.int32),
            (VMEM, acc_shape, full),
        ],
        scratch=(
            VMEM((bodies + 1, width, DEPTH), half),
            VMEM((bodies, 16, width), half),
            VMEM((width, 128), full),
            points,
            SMEM((2, pair_count), jnp.int32),
            SMEM((4,), jnp.int32),
            semaphore,
        ),
        units=3.0,
    )
    first, second = [
        lax.ppermute(
            tiles,
            "body",
            [pair for i in range(start, groups - 1, 2) for pair in ((i, i + 1), (i + 1, i))],
        )
        for start in (0, 1)
    ]
    partial, features = call(
        functools.partial(group_kernel, bodies),
        [(VMEM, codes), (VMEM, tiles), (VMEM, partial)],
        [(VMEM, acc_shape, full), (VMEM, (bodies, rest, DEPTH), half)],
        scratch=(
            VMEM((bodies, 16, rest), half),
            VMEM((rest, 128), full),
            VMEM((rest, DEPTH), half),
            points,
        ),
        units=7.0,
    )
    partner_scratch = (
        VMEM((bodies, wide, DEPTH), half),
        VMEM((bodies, 16, wide), half),
        points,
    )
    partial = call(
        functools.partial(first_partner_kernel, bodies),
        [(VMEM, codes), (VMEM, first), (VMEM, own), (VMEM, partial)],
        [(VMEM, acc_shape, full)],
        scratch=partner_scratch,
        units=2.0,
    )
    potential, force = call(
        functools.partial(second_partner_kernel, bodies),
        [(VMEM, codes), (VMEM, second), (VMEM, own), (VMEM, partial), (VMEM, scaled)],
        [(VMEM, acc_shape, full), (VMEM, (bodies, 8, 128), full)],
        scratch=partner_scratch,
        units=4.0,
    )
    fs_next, own_potential = call(
        functools.partial(velocity_kernel, bodies),
        [(VMEM, tiles), (VMEM, features), (VMEM, velocity), (VMEM, fs_state), (VMEM, potential)],
        [(VMEM, (2, width), full), (HBM, acc_shape, full)],
        scratch=(VMEM((bodies, 16, rest), half), semaphore),
        units=5.0,
    )
    if tiles_count == 4:
        pieces = [force] + rotations(force, "surf")
    else:
        pieces = [lax.psum(force, "surf")] + [jnp.zeros_like(force)] * 3
    total, fs_next = call(
        finish_kernel,
        [(VMEM, piece) for piece in pieces] + [(VMEM, fs_next)],
        [(VMEM, (bodies, 3, 8), full), (VMEM, (2, width), full)],
    )
    return own_potential, total.transpose(0, 2, 1), fs_next


def solution(mesh):
    placed = (
        P(None, "body", "surf"),
        P(None, "body", "surf"),
        P(None, ("body", "surf")),
        P(None, ("body", "surf")),
        P(),
    )
    return jax.shard_map(
        on_device,
        mesh=mesh,
        in_specs=placed,
        out_specs=(P("body", None, "surf"), P("body", None, None), P(None, ("body", "surf"))),
        check_vma=False,
    )
```

```python
import functools

import jax
import jax.numpy as jnp
from jax import lax
from jax.experimental import pallas as pl
from jax.experimental.pallas import tpu as pltpu
from jax.sharding import PartitionSpec as P

soften = 0.01
gravity = 9.81
time_step = 0.2
mid_depth = -1.5
half = jnp.bfloat16
full = jnp.float32
DEPTH = 48


def rows_of(block_shape, rows):
    index = lax.broadcasted_iota(jnp.int32, block_shape, 0)
    block = jnp.zeros(block_shape, full)
    for position, row in enumerate(rows):
        block = jnp.where(index == position, row, block)
    return block


def three_parts(block):
    first = block.astype(half).astype(full)
    rest = block - first
    second = rest.astype(half).astype(full)
    return first, second, rest - second


def source_features(x, y, z):
    norm = x * x + y * y + z * z
    a, b, c = three_parts(rows_of((8, x.shape[1]), (x, y, z, norm, 1.0)))
    return jnp.concatenate([a, b, a, b, c, a], axis=0).astype(half).T


def target_features(x, y, z):
    norm = x * x + y * y + z * z + soften
    a, b, c = three_parts(rows_of((8, x.shape[1]), (-2.0 * x, -2.0 * y, -2.0 * z, 1.0, norm)))
    return jnp.concatenate([a, a, b, b, a, c], axis=0).astype(half)


def two_parts(block):
    first = block.astype(half)
    return first, (block - first.astype(full)).astype(half)


def split_weights(block):
    first = block.astype(half).astype(full)
    return jnp.concatenate([first, block - first], axis=0).astype(half)


def product(left, right):
    return jnp.dot(left, right, preferred_element_type=full)


def weighted_sum(values, weights):
    high, low = two_parts(values)
    both = product(
        jnp.concatenate([weights, weights], axis=1), jnp.concatenate([high, low], axis=0)
    )
    return both[:8] + both[8:]


def influence_sum(targets, sources, weights):
    return weighted_sum(lax.rsqrt(product(sources, targets)), weights)


LANES = 128


def tile_rows(bodies, width):
    return -(-(11 * bodies + 3) * (width // LANES) // 8) * 8


def weight_rows(blocks, member, block):
    start = 8 * (member * blocks + block)
    return slice(start, start + 8)


def entry_row(bodies, blocks, block, entry):
    if entry < 3 * bodies:
        row = 8 * bodies * blocks + 3 * bodies * block + entry
    else:
        row = 11 * bodies * blocks + 3 * block + entry - 3 * bodies
    return slice(row, row + 1)


def tile_entry(tile, bodies, blocks, entry):
    return jnp.concatenate(
        [tile[entry_row(bodies, blocks, block, entry), :] for block in range(blocks)], axis=1
    )


def tile_weights(tile, blocks, member):
    return jnp.concatenate(
        [tile[weight_rows(blocks, member, block), :] for block in range(blocks)], axis=1
    )


def body_points(tile, bodies, blocks, member):
    return [tile_entry(tile, bodies, blocks, 3 * member + axis) for axis in range(3)]


def surface_points(tile, bodies, blocks):
    x, y, weight = [tile_entry(tile, bodies, blocks, 3 * bodies + entry) for entry in range(3)]
    return x, y, jnp.full_like(x, -mid_depth), weight


def shift_kernel(bodies, shift_ref):
    base = lax.axis_index("body") * bodies
    row = lax.broadcasted_iota(jnp.int32, shift_ref.shape, 0)
    shift_ref[...] = jnp.where(row < bodies, 2 * (base + row), 2 * base + bodies - 1).astype(full)


def pack_kernel(shift_ref, panels_ref, surface_ref, tile_ref):
    bodies, width = panels_ref.shape[1:]
    blocks = width // LANES
    if tile_ref.shape[0] > (11 * bodies + 3) * blocks:
        tile_ref[...] = jnp.zeros_like(tile_ref)
    for block in range(blocks):
        lanes = slice(block * LANES, (block + 1) * LANES)
        for member in range(bodies):
            row = slice(member, member + 1)
            area = panels_ref[3, row, lanes]
            rows = weight_rows(blocks, member, block)
            for entry in range(8):
                place = rows.start + entry
                tile_ref[place : place + 1, :] = panels_ref[4 + entry, row, lanes] * area
            for axis, shift in enumerate((shift_ref[row, 0:1], 0.0, mid_depth)):
                tile_ref[entry_row(bodies, blocks, block, 3 * member + axis), :] = (
                    panels_ref[axis, row, lanes] - shift
                )
        surface = (
            surface_ref[0:1, lanes] - shift_ref[bodies : bodies + 1, 0:1],
            surface_ref[1:2, lanes],
            surface_ref[2:3, lanes] * surface_ref[3:4, lanes],
        )
        for entry, value in enumerate(surface):
            tile_ref[entry_row(bodies, blocks, block, 3 * bodies + entry), :] = value


def body_weights(tile, blocks, member):
    return split_weights(tile_weights(tile, blocks, member))


def moment_weights(tile, bodies, blocks, member):
    x, y, z = body_points(tile, bodies, blocks, member)
    first = tile_weights(tile, blocks, member)[0:1, :]
    return split_weights(rows_of((8, x.shape[1]), (first, first * x, first * y, first * z)))


def prepare_tile(tile, bodies, blocks, columns, features, weights, spread):
    for member in range(bodies):
        features[member, columns, :] = source_features(*body_points(tile, bodies, blocks, member))
        weights[member, :, columns] = body_weights(tile, blocks, member)
    x, y, z, weight = surface_points(tile, bodies, blocks)
    features[bodies, columns, :] = source_features(x, y, z)
    spread[columns, :] = jnp.broadcast_to(weight, (128, x.shape[1])).T


def surface_sum(targets, sources, spread):
    values = lax.rsqrt(product(sources, targets))
    count, width = values.shape
    sums = []
    for start in range(0, width, 128):
        term = values[:, start : start + 128] * spread
        sums.append(jnp.sum(term.reshape(count // 8, 8, 128), axis=0))
    return jnp.sum(jnp.concatenate(sums, axis=1), axis=0, keepdims=True)


def velocity_term(features, weights, place, y, z):
    inverse = lax.rsqrt(product(features, target_features(place, y, z)))
    moments = weighted_sum(inverse * inverse * inverse, weights)
    return [
        moments[axis + 1 : axis + 2] - at * moments[0:1] for axis, at in enumerate((place, y, z))
    ]


def targets_of(points, member, shift):
    block = points[member]
    return target_features(block[0:1] + shift, block[1:2], block[2:3])


def code_rows(pair_count):
    return 6 * pair_count + 1


def own_tile_kernel(
    bodies, pairs_hbm, tile_ref, panels_ref, normals_ref, acc_ref, velocity_ref, codes, scaled_ref,
    features, weights, spread, points, pairs, counts, sem,
):
    width = acc_ref.shape[2]
    blocks = width // LANES
    copy = pltpu.make_async_copy(pairs_hbm, pairs, sem)
    copy.start()
    tile = tile_ref[...]
    prepare_tile(tile, bodies, blocks, pl.ds(0, width), features, weights, spread)
    x, y, z, _ = surface_points(tile, bodies, blocks)
    total = [jnp.zeros((1, width), full)] * 3
    index = lax.broadcasted_iota(jnp.int32, (8, width), 0)
    for member in range(bodies):
        point = body_points(tile, bodies, blocks, member)
        points[member] = rows_of((8, width), point)
        self_part = influence_sum(target_features(*point), features[member], weights[member])
        shift = float(2 * member - (bodies - 1))
        surface_part = surface_sum(
            target_features(point[0] + shift, point[1], point[2]), features[bodies], spread[...]
        )
        acc_ref[member] = self_part + jnp.where(index == 0, surface_part, 0.0)
        term = velocity_term(
            features[member], moment_weights(tile, bodies, blocks, member), x - shift, y, z
        )
        total = [so_far + part for so_far, part in zip(total, term)]
    velocity_ref[...] = rows_of((8, width), total)
    for member in range(bodies):
        area = panels_ref[3, member : member + 1, :]
        scaled_ref[member] = rows_of(
            (8, width), [normals_ref[axis, member : member + 1, :] * area for axis in range(3)]
        )

    base = lax.axis_index("body") * bodies
    pair_count = pairs.shape[1]
    copy.wait()
    for entry in range(4):
        counts[entry] = 0

    def list_pair(step, carry):
        low, high = pairs[0, step] - base, pairs[1, step] - base

        @pl.when((high >= 0) & (low < bodies) & ((low >= 0) | (high < bodies)))
        def _():
            inside = (low >= 0) & (high < bodies)
            upper = (low >= 0).astype(jnp.int32)
            target = jnp.where(upper == 1, low, high)
            source = jnp.where(upper == 1, high - jnp.where(inside, 0, bodies), low + bodies)
            partner = 1 - (upper + lax.axis_index("body")) % 2
            row = jnp.where(inside, 0, 1 + partner)
            place = counts[row]
            codes[pl.ds(row * 2 * pair_count + place, 1), :] = jnp.full(
                (1, 128), target * 16 + source, jnp.int32
            )
            counts[row] = place + 1
            counts[3] = counts[3] | jnp.where(
                inside, 0, jnp.left_shift(1, partner * bodies + source)
            )

        return carry

    lax.fori_loop(0, pair_count, list_pair, 0)
    lane = lax.broadcasted_iota(jnp.int32, (1, 128), 1)
    last = jnp.zeros((1, 128), jnp.int32)
    for entry in range(4):
        last = jnp.where(lane == entry, counts[entry], last)
    codes[6 * pair_count : 6 * pair_count + 1, :] = last
    pair_sums(codes, counts[0], points, features, weights, acc_ref)


def over_codes(codes, first, count, visit):
    def step_code(step, code):
        following = codes[first + step + 1, 0]
        visit(code // 16, code % 16)
        return following

    lax.fori_loop(0, count, step_code, codes[first, 0])


def pair_sums(codes, count, points, features, weights, acc_ref):
    def visit(low, high):
        shift = (2 * (low - high)).astype(full)
        to_low = influence_sum(targets_of(points, low, shift), features[high], weights[high])
        to_high = influence_sum(targets_of(points, high, -shift), features[low], weights[low])
        acc_ref[low] += to_low
        acc_ref[high] += to_high

    over_codes(codes, 0, count, visit)


def group_kernel(
    bodies, codes, tiles_ref, given_ref, acc_ref, features, weights, spread, surface, points
):
    count, width = tiles_ref.shape[0], acc_ref.shape[2]
    blocks = width // LANES
    rest = (count - 1) * width
    pair_count = codes.shape[0] // 6
    own = tiles_ref[0]
    for member in range(bodies):
        for index in range(1, count):
            tile = tiles_ref[index]
            columns = pl.ds((index - 1) * width, width)
            features[member, columns, :] = source_features(*body_points(tile, bodies, blocks, member))
            weights[member, :, columns] = body_weights(tile, blocks, member)
        points[member] = rows_of((8, width), body_points(own, bodies, blocks, member))
        acc_ref[member] = given_ref[member] + influence_sum(
            targets_of(points, member, 0.0), features[member], weights[member]
        )
    for index in range(1, count):
        x, y, z, weight = surface_points(tiles_ref[index], bodies, blocks)
        columns = pl.ds((index - 1) * width, width)
        surface[columns, :] = source_features(x, y, z)
        spread[columns, :] = jnp.broadcast_to(weight, (128, width)).T
    for member in range(bodies):
        shift = float(2 * member - (bodies - 1))
        acc_ref[member, 0:1, :] += surface_sum(
            targets_of(points, member, shift), surface[...], spread[...]
        )

    pair_sums(codes, codes[6 * pair_count, 0], points, features, weights, acc_ref)


def partner_sums(bodies, which, codes, side_ref, tile_ref, given_ref, acc_ref, features, weights, points):
    count, width = side_ref.shape[0], acc_ref.shape[2]
    blocks = width // LANES
    pair_count = codes.shape[0] // 6
    crossings = codes[6 * pair_count, 1 + which]
    used = codes[6 * pair_count, 3]
    own = tile_ref[...]
    for member in range(bodies):
        points[member] = rows_of((8, width), body_points(own, bodies, blocks, member))
    acc_ref[...] = given_ref[...]
    for member in range(bodies):

        @pl.when((jnp.right_shift(used, which * bodies + member) & 1) == 1)
        def _():
            for index in range(count):
                columns = pl.ds(index * width, width)
                tile = side_ref[index]
                features[member, columns, :] = source_features(
                    *body_points(tile, bodies, blocks, member)
                )
                weights[member, :, columns] = body_weights(tile, blocks, member)

    upper = (lax.axis_index("body") + which) % 2 == 0
    offset = jnp.where(upper, bodies, -bodies)

    def visit(target, member):
        shift = (2 * (target - member - offset)).astype(full)
        acc_ref[target] += influence_sum(
            targets_of(points, target, shift), features[member], weights[member]
        )

    over_codes(codes, 2 * pair_count * (1 + which), crossings, visit)


def first_partner_kernel(
    bodies, codes, side_ref, tile_ref, given_ref, acc_ref, features, weights, points
):
    partner_sums(
        bodies, 0, codes, side_ref, tile_ref, given_ref, acc_ref, features, weights, points
    )


def second_partner_kernel(
    bodies, codes, side_ref, tile_ref, given_ref, scaled_ref,
    acc_ref, force_ref, features, weights, points,
):
    partner_sums(
        bodies, 1, codes, side_ref, tile_ref, given_ref, acc_ref, features, weights, points
    )
    force_ref[...] = jnp.zeros_like(force_ref)
    for member in range(bodies):
        force_ref[member, :, 0:8] = lax.dot_general(
            scaled_ref[member],
            acc_ref[member],
            (((1,), (1,)), ((), ())),
            precision=lax.Precision.HIGHEST,
            preferred_element_type=full,
        )


def velocity_kernel(
    bodies, tiles_ref, features, given_ref, state_ref, potential_ref, next_ref, potential_hbm, weights, sem
):
    count, width = tiles_ref.shape[0], next_ref.shape[1]
    blocks = width // LANES
    rest = (count - 1) * width
    store = pltpu.make_async_copy(potential_ref, potential_hbm, sem)
    store.start()
    for index in range(1, count):
        tile = tiles_ref[index]
        for member in range(bodies):
            weights[member, :, pl.ds((index - 1) * width, width)] = moment_weights(
                tile, bodies, blocks, member
            )
    own = tiles_ref[0]
    x, y, z, _ = surface_points(own, bodies, blocks)

    velocity = [given_ref[axis : axis + 1, :] for axis in range(3)]
    for member in range(bodies):
        place = x + float(bodies - 1 - 2 * member)
        term = velocity_term(features[member], weights[member], place, y, z)
        velocity = [so_far + part for so_far, part in zip(velocity, term)]
    speed_sq = velocity[0] * velocity[0] + velocity[1] * velocity[1] + velocity[2] * velocity[2]
    potential, elevation = state_ref[0:1, :], state_ref[1:2, :]
    next_ref[0:1, :] = potential + time_step * (-gravity * elevation - 0.5 * speed_sq)
    next_ref[1:2, :] = elevation + time_step * velocity[2]
    store.wait()


def finish_kernel(own_ref, third_ref, second_ref, first_ref, next_ref, force_ref, out_ref):
    total = (own_ref[...] + second_ref[...]) + (first_ref[...] + third_ref[...])
    force_ref[...] = total[:, :3, :8]
    out_ref[...] = next_ref[...]


VMEM, SMEM, HBM = pltpu.VMEM, pltpu.SMEM, pltpu.HBM


def call(kernel, operands, results, scratch=(), units=0.0):
    single = len(results) == 1
    out = pl.pallas_call(
        kernel,
        out_shape=[jax.ShapeDtypeStruct(shape, kind) for _, shape, kind in results],
        in_specs=[pl.BlockSpec(memory_space=space) for space, _ in operands],
        out_specs=[pl.BlockSpec(memory_space=space) for space, _, _ in results],
        scratch_shapes=list(scratch),
        compiler_params=pltpu.CompilerParams(vmem_limit_bytes=40 * 1024 * 1024),
        cost_estimate=pl.CostEstimate(
            flops=int(units * 1.2e9), bytes_accessed=1024, transcendentals=0
        ),
    )(*[array for _, array in operands])
    return out[0] if single else out


def rotations(block, axis):
    count = lax.axis_size(axis)
    return [
        lax.ppermute(block, axis, [(i, (i + k) % count) for i in range(count)])
        for k in range(1, count)
    ]


def exchanges(block, axis):
    count = lax.axis_size(axis)
    return [lax.ppermute(block, axis, [(i, i ^ k) for i in range(count)]) for k in range(1, count)]


def on_device(body_panels, body_normals, fs_panels, fs_state, pairs):
    bodies = body_panels.shape[1]
    width = body_panels.shape[2]
    tiles_count = lax.axis_size("surf")
    groups = lax.axis_size("body")
    pair_count = pairs.shape[0]
    semaphore = pltpu.SemaphoreType.DMA
    shifts = call(
        functools.partial(shift_kernel, bodies), [], [(VMEM, (8, 128), full)], units=2.0
    )
    own = call(
        pack_kernel,
        [(VMEM, shifts), (VMEM, body_panels), (VMEM, fs_panels)],
        [(VMEM, (tile_rows(bodies, width), LANES), full)],
    )
    if tiles_count == 4:
        tiles = jnp.stack([own] + exchanges(own, "surf"))
    else:
        everything = lax.all_gather(own, "surf")
        tiles = jnp.concatenate(
            [own[None]]
            + [
                lax.dynamic_index_in_dim(
                    everything, (lax.axis_index("surf") + k) % tiles_count, 0
                )
                for k in range(1, tiles_count)
            ]
        )
    wide = width * tiles_count
    rest = wide - width
    acc_shape = (bodies, 8, width)
    points = VMEM(acc_shape, full)
    partial, velocity, codes, scaled = call(
        functools.partial(own_tile_kernel, bodies),
        [(HBM, pairs.T), (VMEM, own), (VMEM, body_panels), (VMEM, body_normals)],
        [
            (VMEM, acc_shape, full),
            (VMEM, (8, width), full),
            (VMEM, (code_rows(pair_count), 128), jnp.int32),
            (VMEM, acc_shape, full),
        ],
        scratch=(
            VMEM((bodies + 1, width, DEPTH), half),
            VMEM((bodies, 16, width), half),
            VMEM((width, 128), full),
            points,
            SMEM((2, pair_count), jnp.int32),
            SMEM((4,), jnp.int32),
            semaphore,
        ),
        units=3.0,
    )
    near = tiles[:, : -(-11 * bodies * (width // LANES) // 8) * 8]
    first, second = [
        lax.ppermute(
            near,
            "body",
            [pair for i in range(start, groups - 1, 2) for pair in ((i, i + 1), (i + 1, i))],
        )
        for start in (0, 1)
    ]
    partial, features = call(
        functools.partial(group_kernel, bodies),
        [(VMEM, codes), (VMEM, tiles), (VMEM, partial)],
        [(VMEM, acc_shape, full), (VMEM, (bodies, rest, DEPTH), half)],
        scratch=(
            VMEM((bodies, 16, rest), half),
            VMEM((rest, 128), full),
            VMEM((rest, DEPTH), half),
            points,
        ),
        units=7.0,
    )
    partner_scratch = (
        VMEM((bodies, wide, DEPTH), half),
        VMEM((bodies, 16, wide), half),
        points,
    )
    partial = call(
        functools.partial(first_partner_kernel, bodies),
        [(VMEM, codes), (VMEM, first), (VMEM, own), (VMEM, partial)],
        [(VMEM, acc_shape, full)],
        scratch=partner_scratch,
        units=2.0,
    )
    potential, force = call(
        functools.partial(second_partner_kernel, bodies),
        [(VMEM, codes), (VMEM, second), (VMEM, own), (VMEM, partial), (VMEM, scaled)],
        [(VMEM, acc_shape, full), (VMEM, (bodies, 8, 128), full)],
        scratch=partner_scratch,
        units=4.0,
    )
    fs_next, own_potential = call(
        functools.partial(velocity_kernel, bodies),
        [(VMEM, tiles), (VMEM, features), (VMEM, velocity), (VMEM, fs_state), (VMEM, potential)],
        [(VMEM, (2, width), full), (HBM, acc_shape, full)],
        scratch=(VMEM((bodies, 16, rest), half), semaphore),
        units=5.0,
    )
    if tiles_count == 4:
        pieces = [force] + rotations(force, "surf")[::-1]
    else:
        pieces = [lax.psum(force, "surf")] + [jnp.zeros_like(force)] * 3
    total, fs_next = call(
        finish_kernel,
        [(VMEM, piece) for piece in pieces] + [(VMEM, fs_next)],
        [(VMEM, (bodies, 3, 8), full), (VMEM, (2, width), full)],
    )
    return own_potential, total.transpose(0, 2, 1), fs_next


def solution(mesh):
    placed = (
        P(None, "body", "surf"),
        P(None, "body", "surf"),
        P(None, ("body", "surf")),
        P(None, ("body", "surf")),
        P(),
    )
    return jax.shard_map(
        on_device,
        mesh=mesh,
        in_specs=placed,
        out_specs=(P("body", None, "surf"), P("body", None, None), P(None, ("body", "surf"))),
        check_vma=False,
    )
```
